32 devices in a mesh: fsdp: 8 (over z, y), rep: 4 (over x, core).
Axes of the slice: x: 2, y: 2, z: 4, core: 2. Of those that a mesh axis runs over, the one named last changes fastest.
Arguments:
- tokens: bfloat16 [32, 1024, 768], P(('fsdp', 'rep')), may hold values from -6 to 6
- cotangent: bfloat16 [32, 1024, 768], P(('fsdp', 'rep')), may hold values from -6 to 6
- seq_lengths: int32 [32], P(('fsdp', 'rep')), may hold values from 256 to 1024, as said below
- token_positions: int32 [32, 1024], P(('fsdp', 'rep')), may hold values from 0 to 2046, as said below
- first_query: bfloat16 [768, 768], P('fsdp'), may hold values from -0.21875 to 0.21875
- first_key: bfloat16 [768, 768], P('fsdp'), may hold values from -0.21875 to 0.21875
- first_value: bfloat16 [768, 768], P('fsdp'), may hold values from -0.21875 to 0.21875
- first_output: bfloat16 [768, 768], P('fsdp'), may hold values from -1.75 to 1.75
- first_gate: bfloat16 [768, 2048], P('fsdp'), may hold values from -0.21875 to 0.21875
- first_up: bfloat16 [768, 2048], P('fsdp'), may hold values from -0.21875 to 0.21875
- first_down: bfloat16 [2048, 768], P('fsdp'), may hold values from -0.125 to 0.125
- first_attngain: bfloat16 [768], P('fsdp'), may hold values from 0.099609375 to 1.8984375
- first_ffngain: bfloat16 [768], P('fsdp'), may hold values from 0.099609375 to 1.8984375
- second_query: bfloat16 [768, 768], P('fsdp'), may hold values from -0.21875 to 0.21875
- second_key: bfloat16 [768, 768], P('fsdp'), may hold values from -0.21875 to 0.21875
- second_value: bfloat16 [768, 768], P('fsdp'), may hold values from -0.21875 to 0.21875
- second_output: bfloat16 [768, 768], P('fsdp'), may hold values from -1.75 to 1.75
- second_gate: bfloat16 [768, 2048], P('fsdp'), may hold values from -0.21875 to 0.21875
- second_up: bfloat16 [768, 2048], P('fsdp'), may hold values from -0.21875 to 0.21875
- second_down: bfloat16 [2048, 768], P('fsdp'), may hold values from -0.125 to 0.125
- second_attngain: bfloat16 [768], P('fsdp'), may hold values from 0.099609375 to 1.8984375
- second_ffngain: bfloat16 [768], P('fsdp'), may hold values from 0.099609375 to 1.8984375
Outputs:
- first_hidden: float32 [32, 1024, 768], P(('fsdp', 'rep'))
- second_hidden: float32 [32, 1024, 768], P(('fsdp', 'rep'))
- input_grad: float32 [32, 1024, 768], P(('fsdp', 'rep'))
- first_query_grad: float32 [768, 768], P('fsdp')
- first_key_grad: float32 [768, 768], P('fsdp')
- first_value_grad: float32 [768, 768], P('fsdp')
- first_output_grad: float32 [768, 768], P('fsdp')
- first_gate_grad: float32 [768, 2048], P('fsdp')
- first_up_grad: float32 [768, 2048], P('fsdp')
- first_down_grad: float32 [2048, 768], P('fsdp')
- first_attngain_grad: float32 [768], P('fsdp')
- first_ffngain_grad: float32 [768], P('fsdp')
- second_query_grad: float32 [768, 768], P('fsdp')
- second_key_grad: float32 [768, 768], P('fsdp')
- second_value_grad: float32 [768, 768], P('fsdp')
- second_output_grad: float32 [768, 768], P('fsdp')
- second_gate_grad: float32 [768, 2048], P('fsdp')
- second_up_grad: float32 [768, 2048], P('fsdp')
- second_down_grad: float32 [2048, 768], P('fsdp')
- second_attngain_grad: float32 [768], P('fsdp')
- second_ffngain_grad: float32 [768], P('fsdp')
The draws below stay inside these ranges and needn't reach their ends.
Inputs may be any that keep to these rules, and one draw needn't show every extreme that they name: `seq_lengths`: keys at or past a sequence's length are masked; some sequence is 1024 long and some 1024/4. `token_positions`: each sequence starts at 0 and rises by 1 or 2 from token to token.
All inputs are finite; a program needn't handle non-finite values.
Results may differ from the reference program's by a relative error of at most 0.034.
Values may be sent and summed in bfloat16 or wider, within the bound.
No kernel may reach another device: no remote copies, remote signals or barrier semaphores. Data moves between devices by JAX's collectives and lax.ppermute only.
A program may use at most 384 MiB of HBM per device.

```python
import math
import jax
import jax.numpy as jnp
from jax import lax

D = 768
FF = 2048
HEADS = 12
HEAD_DIM = 64
LEN = 1024
SEQS = 32


def draw_seq_lengths(key, part):
    key = jax.random.fold_in(key, 11)
    key_lengths, key_top, key_low = jax.random.split(key, 3)
    lengths = jax.random.randint(key_lengths, (SEQS,), LEN // 4, LEN + 1)
    chosen_top = jax.random.randint(key_top, (), 0, SEQS)
    chosen_low = (chosen_top + 1 + jax.random.randint(key_low, (), 0, SEQS - 1)) % SEQS
    lengths = lengths.at[chosen_top].set(LEN)
    lengths = lengths.at[chosen_low].set(LEN // 4)
    return lengths.astype(jnp.int32)


def draw_token_positions(key, part):
    key = jax.random.fold_in(key, 23)
    key_steps, key_row = jax.random.split(key)
    strides = jax.random.randint(key_steps, (SEQS, LEN), 1, 3)
    chosen_row = jax.random.randint(key_row, (), 0, SEQS)
    row_index = jnp.arange(SEQS)[:, None]
    strides = jnp.where(row_index == chosen_row, 2, strides)
    strides = strides.at[:, 0].set(0)
    return jnp.cumsum(strides, axis=1).astype(jnp.int32)


def spiked(values, key, source, target, blocks, factor):
    owner, partner = [(jnp.arange(values.shape[dim]) // (values.shape[dim] // blocks)).reshape([-1 if axis == dim else 1 for axis in range(values.ndim)]) for dim in (source, target)]
    chosen = jax.random.permutation(key, blocks)[partner]
    strong = (owner == chosen) | (owner == (partner + blocks // 2) % blocks)
    return jnp.where(strong, factor * values, values)


def levels(stream_key, shape, cuts, low, largest):
    def one(axis_at, shards_of):
        heights = jax.random.uniform(jax.random.fold_in(jax.random.fold_in(stream_key, 6), axis_at), (shards_of,), jnp.float32, low / len(cuts), largest / len(cuts))
        return jnp.repeat(jnp.exp(heights), shape[axis_at] // shards_of).reshape((-1,) + (1,) * (len(shape) - axis_at - 1))

    factor_of = one(*cuts[0])
    for cut in cuts[1:]:
        factor_of = factor_of * one(*cut)
    return factor_of


def normal_values(stream_key, shape, spread, most, cuts=(), held_as=jnp.bfloat16):
    values = spread * jax.random.normal(stream_key, shape, jnp.float32)
    if cuts:
        values = values * levels(stream_key, shape, cuts, -0.22, 0.18)
    return jnp.clip(values, -most, most).astype(held_as)


def bell_draw_with(own_key, dims, spread, reach, pieces, heavy, dtype=jnp.bfloat16):
    drawn = spread * jax.random.normal(own_key, dims, jnp.float32)
    if pieces:
        drawn = drawn * levels(own_key, dims, pieces, -0.22, 0.18)
    return jnp.clip(spiked(drawn, jax.random.fold_in(own_key, 3), *heavy), -reach, reach).astype(dtype)


def setup_inputs(seed: int = 0) -> dict:
    keys = jax.random.split(jax.random.key(seed), 23)
    tokens = normal_values(keys[0], (SEQS, LEN, D), 1.0, 6.0, ((0, 32),))
    cotangent = bell_draw_with(keys[1], (SEQS, LEN, D), 1.0, 6.0, ((0, 32),), (0, 2, 32, 2.75))
    seq_lengths = draw_seq_lengths(jax.random.fold_in(keys[22], 71), 0)
    token_positions = draw_token_positions(jax.random.fold_in(keys[22], 71), 0)
    first_query = normal_values(keys[4], (D, D), D ** -0.5, 0.21875, ((0, 8),))
    first_key = normal_values(keys[5], (D, D), D ** -0.5, 0.21875, ((0, 8),))
    first_value = normal_values(keys[6], (D, D), D ** -0.5, 0.21875, ((0, 8),))
    first_output = normal_values(keys[7], (D, D), (D // 64) ** -0.5, 1.75, ((0, 8),))
    first_gate = normal_values(keys[8], (D, FF), D ** -0.5, 0.21875, ((0, 8),))
    first_up = normal_values(keys[9], (D, FF), D ** -0.5, 0.21875, ((0, 8),))
    first_down = normal_values(keys[10], (FF, D), FF ** -0.5, 0.125, ((0, 8),))
    first_attngain = jnp.clip(1.0 + 0.18 * jax.random.normal(keys[11], (D,), jnp.float32), 0.099609375, 1.8984375).astype(jnp.bfloat16)
    first_ffngain = jnp.clip(1.0 + 0.18 * jax.random.normal(keys[12], (D,), jnp.float32), 0.099609375, 1.8984375).astype(jnp.bfloat16)
    second_query = normal_values(keys[13], (D, D), D ** -0.5, 0.21875, ((0, 8),))
    second_key = normal_values(keys[14], (D, D), D ** -0.5, 0.21875, ((0, 8),))
    second_value = normal_values(keys[15], (D, D), D ** -0.5, 0.21875, ((0, 8),))
    second_output = normal_values(keys[16], (D, D), (D // 64) ** -0.5, 1.75, ((0, 8),))
    second_gate = normal_values(keys[17], (D, FF), D ** -0.5, 0.21875, ((0, 8),))
    second_up = normal_values(keys[18], (D, FF), D ** -0.5, 0.21875, ((0, 8),))
    second_down = normal_values(keys[19], (FF, D), FF ** -0.5, 0.125, ((0, 8),))
    second_attngain = jnp.clip(1.0 + 0.18 * jax.random.normal(keys[20], (D,), jnp.float32), 0.099609375, 1.8984375).astype(jnp.bfloat16)
    second_ffngain = jnp.clip(1.0 + 0.18 * jax.random.normal(keys[21], (D,), jnp.float32), 0.099609375, 1.8984375).astype(jnp.bfloat16)
    return dict(tokens=tokens, cotangent=cotangent, seq_lengths=seq_lengths, token_positions=token_positions, first_query=first_query, first_key=first_key, first_value=first_value, first_output=first_output, first_gate=first_gate, first_up=first_up, first_down=first_down, first_attngain=first_attngain, first_ffngain=first_ffngain, second_query=second_query, second_key=second_key, second_value=second_value, second_output=second_output, second_gate=second_gate, second_up=second_up, second_down=second_down, second_attngain=second_attngain, second_ffngain=second_ffngain)


epsilon = 1e-06
masked_score = -1e+30
highest = lax.Precision.HIGHEST

@jax.custom_vjp
def low(v):
    return lax.optimization_barrier(v.astype(jnp.bfloat16)).astype(jnp.float32)

@jax.custom_vjp
def low_back(v):
    return v

def low_keep(v):
    return (low(v), None)

def low_pass(kept, grad):
    return (grad,)

def back_keep(v):
    return (v, None)

def back_low(kept, grad):
    return (low(grad),)
low.defvjp(low_keep, low_pass)
low_back.defvjp(back_keep, back_low)

def rms_norm(values, scales):
    return values * lax.rsqrt(lax.optimization_barrier(jnp.mean(values * values, axis=-1, keepdims=True)) + epsilon) * scales

def project(inputs, matrix):
    return jnp.einsum('bte,ef->btf', inputs, matrix, precision=highest)

def rotate(values, cosine, sine_table):
    middle = values.shape[-1] // 2
    turned = jnp.concatenate([-values[..., middle:], values[..., :middle]], axis=-1)
    return values * cosine + turned * sine_table

def rope_tables(positions):
    even_steps = jnp.arange(0, HEAD_DIM, 2).astype(jnp.float32)
    inverse = jnp.exp(even_steps * (-math.log(10000.0) / HEAD_DIM))
    angles = positions.astype(jnp.float32)[..., None] * inverse
    cosine = jnp.concatenate([jnp.cos(angles), jnp.cos(angles)], axis=-1)[..., None, :]
    sine_table = jnp.concatenate([jnp.sin(angles), jnp.sin(angles)], axis=-1)[..., None, :]
    return (cosine, sine_table)

def split_heads(values):
    return values.reshape(values.shape[0], values.shape[1], HEADS, HEAD_DIM)

def attention(inputs, query_w, key_w, value_w, output_w, cosine, sine_table, lengths):
    queries = low(rotate(split_heads(low_back(project(inputs, query_w))), cosine, sine_table))
    key_rows = low(rotate(split_heads(low_back(project(inputs, key_w))), cosine, sine_table))
    value_rows = split_heads(low(low_back(project(inputs, value_w))))
    scores = low_back(jnp.einsum('bqhd,bkhd->bhqk', queries, key_rows, precision=highest) * HEAD_DIM ** (-0.5))
    position = jnp.arange(LEN)
    causal = position[None, :] <= position[:, None]
    inside = position[None, :] < lengths[:, None]
    valid = causal[None, None] & inside[:, None, None, :]
    scores = jnp.where(valid, scores, masked_score)
    attention_weights = jax.nn.softmax(scores, axis=-1)
    mixed = jnp.einsum('bhqk,bkhd->bqhd', low(attention_weights), value_rows, precision=highest)
    mixed = mixed.reshape(mixed.shape[0], LEN, D)
    return low_back(project(low(low_back(mixed)), output_w))

def feed_forward(inputs, gate_w, up_w, down_w):
    gated = low_back(project(inputs, gate_w))
    upward = low_back(project(inputs, up_w))
    return low_back(project(low(jax.nn.silu(gated) * upward), down_w))

def forward(tokens_in, params, cosine, sine_table, lengths):
    query_a, key_a, value_a, output_a, gate_a, up_a, down_a, attn_a, ffn_a, query_b, key_b, value_b, output_b, gate_b, up_b, down_b, attn_b, ffn_b = params
    resid_one = tokens_in + attention(tokens_in, query_a, key_a, value_a, output_a, cosine, sine_table, lengths)
    normed = rms_norm(resid_one, attn_a)
    first_out = rms_norm(normed + feed_forward(low(normed), gate_a, up_a, down_a), ffn_a)
    resid_two = first_out + attention(low(rms_norm(first_out, attn_b)), query_b, key_b, value_b, output_b, cosine, sine_table, lengths)
    second = resid_two + feed_forward(low(rms_norm(resid_two, ffn_b)), gate_b, up_b, down_b)
    return (second, first_out)

def reference(tokens, cotangent, seq_lengths, token_positions, first_query, first_key, first_value, first_output, first_gate, first_up, first_down, first_attngain, first_ffngain, second_query, second_key, second_value, second_output, second_gate, second_up, second_down, second_attngain, second_ffngain):
    params = tuple((weight.astype(jnp.float32) for weight in (first_query, first_key, first_value, first_output, first_gate, first_up, first_down, first_attngain, first_ffngain, second_query, second_key, second_value, second_output, second_gate, second_up, second_down, second_attngain, second_ffngain)))
    per_block = math.gcd(SEQS, max(1, 4096 // LEN))
    blocks = SEQS // per_block

    def regroup(array):
        return array.reshape((blocks, per_block) + array.shape[1:])

    def one_block(totals, sequence):
        block_tokens, block_cot, block_lengths, block_positions = sequence
        cosine, sine_table = rope_tables(block_positions)

        def apply(tokens_in, weights):
            return forward(tokens_in, weights, cosine, sine_table, block_lengths)
        second, backward, first_out = jax.vjp(apply, block_tokens.astype(jnp.float32), params, has_aux=True)
        tokens_grad, weight_grads = backward(block_cot.astype(jnp.float32))
        totals = tuple((total + grad_one for total, grad_one in zip(totals, weight_grads)))
        return (totals, (first_out, second, tokens_grad))
    starting = tuple((jnp.zeros_like(weight) for weight in params))
    totals, (first_out, second, tokens_grad) = lax.scan(one_block, starting, (regroup(tokens), regroup(cotangent), regroup(seq_lengths), regroup(token_positions)))

    def flatten(array):
        return array.reshape((SEQS,) + array.shape[2:])
    return (flatten(first_out), flatten(second), flatten(tokens_grad), totals[0], totals[1], totals[2], totals[3], totals[4], totals[5], totals[6], totals[7], totals[8], totals[9], totals[10], totals[11], totals[12], totals[13], totals[14], totals[15], totals[16], totals[17])
```

```python
import functools
import math

import jax
import jax.numpy as jnp
from jax import lax
from jax.experimental import pallas as pl
from jax.experimental.pallas import tpu as pltpu
from jax.sharding import PartitionSpec as P

HEAD_DIM = 64

epsilon = 1e-06
masked_score = -1e30


class Grid:
    def __init__(self, fsdp, rep):
        self.zs = fsdp // 2
        self.rep = rep

    def flat(self, z, y, x, c):
        return (z * 2 + y) * self.rep + x * 2 + c

    def pairs(self, move):
        out = []
        for z in range(self.zs):
            for y in range(2):
                for x in range(2):
                    for c in range(2):
                        out.append((self.flat(z, y, x, c), self.flat(*move(z, y, x, c))))
        return out


AXES = ("fsdp", "rep")


def send(grid, value, move):
    return lax.ppermute(value, AXES, grid.pairs(move))


def first_flip(z, y, x, c):
    return (z, y, 1 - x, c) if c == 0 else (z, 1 - y, x, c)


def second_flip(z, y, x, c):
    return (z, 1 - y, x, c) if c == 0 else (z, y, 1 - x, c)


def core_flip(z, y, x, c):
    return (z, y, x, 1 - c)


def x_flip(z, y, x, c):
    return (z, y, 1 - x, c)


def y_flip(z, y, x, c):
    return (z, 1 - y, x, c)

BLOCK = 256
PAIR = 2 * HEAD_DIM
VMEM = 60 * 1024 * 1024
F32 = jnp.float32
LOW = jnp.bfloat16


def dot(one, two):
    return jnp.dot(one, two, preferred_element_type=F32)


def dot_nt(one, two):
    return lax.dot_general(one, two, (((1,), (1,)), ((), ())), preferred_element_type=F32)


def dot_tn(one, two):
    return lax.dot_general(one, two, (((0,), (0,)), ((), ())), preferred_element_type=F32)


def inverse_rms(values):
    return lax.rsqrt(jnp.mean(values * values, axis=-1, keepdims=True) + epsilon)


def norm_back(values, scales, upstream):
    inv = inverse_rms(values)
    weighted = upstream * scales
    inner = jnp.mean(weighted * values, axis=-1, keepdims=True)
    return inv * weighted - values * (inv * inv * inv) * inner, upstream * values * inv


def fold_rows(values):
    return jnp.sum(values.reshape(values.shape[0] // 8, 8, values.shape[1]), axis=0)


def silu_parts(gate):
    sig = 1.0 / (1.0 + jnp.exp(-gate))
    return sig, gate * sig


def piece_place(at_ref, which, k, zs):
    z, y, x, c = at_ref[0], at_ref[1], at_ref[2], at_ref[3]
    cc = c if which < 4 else 1 - c
    first, second = which % 2, (which % 4) // 2
    flip_x = jnp.where(cc == 0, first, second)
    flip_y = jnp.where(cc == 0, second, first)
    zz = lax.rem(z + zs - k, zs)
    return zz * 2 + jnp.where(flip_y == 1, 1 - y, y), jnp.where(flip_x == 1, 1 - x, x), cc


def weight_copies(at_ref, pieces, w_ref, sems):
    if len(pieces) == 1:
        return [pltpu.make_async_copy(pieces[0], w_ref, sems.at[0])]
    zs, rows, _ = pieces[0].shape
    copies = []
    for which in range(8):
        for k in range(zs):
            shard, x, c = piece_place(at_ref, which, k, zs)
            row = pl.multiple_of(shard * (2 * rows) + x * rows, 16)
            copies.append(
                pltpu.make_async_copy(
                    pieces[which].at[k],
                    w_ref.at[c, pl.ds(row, rows), :],
                    sems.at[which * zs + k],
                )
            )
    return copies


def weight_shape(pieces):
    if len(pieces) == 1:
        return pieces[0].shape
    zs, rows, cols = pieces[0].shape
    return (2, zs * 4 * rows, cols)


def weight_scratch(pieces):
    copies = 1 if len(pieces) == 1 else 8 * pieces[0].shape[0]
    return [pltpu.VMEM(weight_shape(pieces), LOW), pltpu.SemaphoreType.DMA((copies,))]


def load_first(at_ref, *weights):
    @pl.when(pl.program_id(0) == 0)
    def _():
        copies = []
        for pieces, w_ref, sems in weights:
            copies += weight_copies(at_ref, pieces, w_ref, sems)
        for copy in copies:
            copy.start()
        for copy in copies:
            copy.wait()


ANYWHERE = pl.BlockSpec(memory_space=pl.ANY)


def rows_spec(cols, block=BLOCK):
    return pl.BlockSpec((block, cols), lambda i, at: (i, 0))


def whole_spec(shape):
    return pl.BlockSpec(shape, lambda i, at: (0,) * len(shape))


def pair_spec(rows, first_pair):
    return pl.BlockSpec((rows, PAIR), lambda p, at: (0, p + first_pair))


def logs_spec(rows, first_pair):
    return pl.BlockSpec((1, 16, rows), lambda p, at: (p + first_pair, 0, 0))


def call(kernel, at, arrays, specs, outs, out_specs, scratch, steps, micros=10.0, aliases={}):
    return pl.pallas_call(
        kernel,
        out_shape=outs,
        grid_spec=pltpu.PrefetchScalarGridSpec(
            num_scalar_prefetch=1,
            grid=(steps,),
            in_specs=specs,
            out_specs=out_specs,
            scratch_shapes=scratch,
        ),
        input_output_aliases=aliases,
        compiler_params=pltpu.CompilerParams(vmem_limit_bytes=VMEM),
        cost_estimate=pl.CostEstimate(
            flops=int(micros * 1.1e9), bytes_accessed=int(micros * 1e5), transcendentals=0
        ),
    )(at, *arrays)


def shape_of(shape, dtype):
    return jax.ShapeDtypeStruct(shape, dtype)


def turn_lanes(values, lane):
    return jnp.where(
        (lane & (HEAD_DIM - 1)) < HEAD_DIM // 2,
        pltpu.roll(values, PAIR - HEAD_DIM // 2, 1),
        pltpu.roll(values, HEAD_DIM // 2, 1),
    )


def project_heads(at, inputs, pieces, cosine, sine):
    rows, width = inputs.shape
    half = width // 2
    n = len(pieces)

    def kernel(at_ref, a_ref, cos_ref, sin_ref, *refs):
        parts, (q_ref, k_ref, v_ref), (w_ref, sems) = refs[:n], refs[n : n + 3], refs[n + 3 :]
        load_first(at_ref, (parts, w_ref, sems))
        a = a_ref[...]
        cos, sin = cos_ref[...], sin_ref[...]
        lane = lax.broadcasted_iota(jnp.int32, (BLOCK, PAIR), 1)
        for c in range(2):
            res = dot(a, w_ref[c])
            for t in range(half // PAIR):
                here = slice(c * half + t * PAIR, c * half + (t + 1) * PAIR)
                q = res[:, t * PAIR : (t + 1) * PAIR]
                k = res[:, half + t * PAIR : half + (t + 1) * PAIR]
                q = q * cos + turn_lanes(q, lane) * sin
                q_ref[:, here] = (q * HEAD_DIM**-0.5).astype(LOW)
                k_ref[:, here] = (k * cos + turn_lanes(k, lane) * sin).astype(LOW)
            v_ref[:, c * half : (c + 1) * half] = res[:, 2 * half :].astype(LOW)

    return call(
        kernel,
        at,
        [inputs, cosine, sine, *pieces],
        [rows_spec(width), rows_spec(PAIR), rows_spec(PAIR)] + [ANYWHERE] * n,
        [shape_of((rows, width), LOW)] * 3,
        [rows_spec(width)] * 3,
        weight_scratch(pieces),
        rows // BLOCK,
        10,
    )


def head_masks(head, lane):
    own = lane < HEAD_DIM if head == 0 else lane >= HEAD_DIM
    return own, lane == (HEAD_DIM if head == 0 else 0)


def attend(at, queries, key_rows, value_rows, first_pair, pairs, before=()):
    rows, width = queries.shape
    every = width // PAIR

    def kernel(at_ref, q_ref, k_ref, v_ref, *refs):
        o_ref, lse_ref = refs[len(before) :]
        lane = lax.broadcasted_iota(jnp.int32, (rows, PAIR), 1)
        row = lax.broadcasted_iota(jnp.int32, (rows, PAIR), 0)
        bias = jnp.where(row < at_ref[4], 0.0, masked_score)
        q, k, v = q_ref[...].astype(F32), k_ref[...].astype(F32), v_ref[...].astype(F32)
        below = lax.broadcasted_iota(jnp.int32, (BLOCK, BLOCK), 0) >= lax.broadcasted_iota(
            jnp.int32, (BLOCK, BLOCK), 1
        )
        heads = []
        for head in range(2):
            own, mark = head_masks(head, lane)
            heads.append(
                (
                    jnp.where(own, q, jnp.where(mark, 1.0, 0.0)).astype(LOW),
                    jnp.where(own, k, jnp.where(mark, bias, 0.0)).astype(LOW),
                    jnp.where(own, v, 1.0).astype(LOW),
                )
            )
        lane_here = lane[:BLOCK]
        for first in range(0, rows, BLOCK):
            end = first + BLOCK
            mixed, logs = [], []
            for qh, kh, vh in heads:
                scores = dot_nt(qh[first:end], kh[:end])
                edge = jnp.where(below, scores[:, first:], masked_score)
                scores = jnp.concatenate([scores[:, :first], edge], axis=1) if first else edge
                top = jnp.max(scores, axis=-1, keepdims=True)
                weights = jnp.exp(scores - top).astype(LOW)
                both = dot(weights, vh[:end])
                total = pltpu.roll(both, HEAD_DIM, 1)
                mixed.append(both / total)
                logs.append(top + jnp.log(total))
            o_ref[first:end, :] = jnp.where(lane_here < HEAD_DIM, mixed[0], mixed[1]).astype(LOW)
            turned = jnp.where(lane_here < HEAD_DIM, logs[0], logs[1]).T
            lse_ref[0, 0:8, first:end] = turned[0:8]
            lse_ref[0, 8:16, first:end] = turned[HEAD_DIM : HEAD_DIM + 8]

    return call(
        kernel,
        at,
        [queries, key_rows, value_rows, *before],
        [pair_spec(rows, first_pair)] * 3 + [ANYWHERE] * len(before),
        [shape_of((rows, width), LOW), shape_of((every, 16, rows), F32)],
        [pair_spec(rows, first_pair), logs_spec(rows, first_pair)],
        [],
        pairs,
        4 * pairs,
        {4 + i: i for i in range(len(before))},
    )


def attend_back(
    at, queries, key_rows, value_rows, mixed, logs, upstream, cosine, sine, first_pair, pairs, before=()
):
    rows, width = queries.shape

    def kernel(at_ref, q_ref, k_ref, v_ref, o_ref, lse_ref, g_ref, cos_ref, sin_ref, *refs):
        dq_ref, dk_ref, dv_ref, sum_ref = refs[len(before) :]
        lane = lax.broadcasted_iota(jnp.int32, (rows, PAIR), 1)
        row = lax.broadcasted_iota(jnp.int32, (rows, PAIR), 0)
        bias = jnp.where(row < at_ref[4], 0.0, masked_score)
        q, k, v = q_ref[...].astype(F32), k_ref[...].astype(F32), v_ref[...].astype(F32)
        q_low, k_low, g_low = q_ref[...], k_ref[...], g_ref[...]
        above = lax.broadcasted_iota(jnp.int32, (BLOCK, BLOCK), 0) <= lax.broadcasted_iota(
            jnp.int32, (BLOCK, BLOCK), 1
        )
        turned = (g_low.astype(F32) * o_ref[...].astype(F32)).T
        cos, sin = cos_ref[...], sin_ref[...]

        def unrotate(values, first, end):
            moved = values * sin[first:end]
            return values * cos[first:end] + turn_lanes(moved, lane[first:end])

        key_parts, value_parts = [], []
        for head in range(2):
            own, mark = head_masks(head, lane)
            qh = jnp.where(own, q, jnp.where(mark, 1.0, 0.0)).astype(LOW)
            kh = jnp.where(own, k, jnp.where(mark, bias, 0.0)).astype(LOW)
            vh = jnp.where(own, v, 0.0).astype(LOW)
            delta = jnp.sum(
                turned[head * HEAD_DIM : (head + 1) * HEAD_DIM], axis=0, keepdims=True
            )
            lse = lse_ref[0, head * 8 : head * 8 + 1, :]
            key_parts.append([])
            value_parts.append([])
            for first in range(0, rows, BLOCK):
                end = first + BLOCK
                scores = dot_nt(kh[first:end], qh[first:])
                soft = jnp.exp(scores - lse[:, first:])
                edge = jnp.where(above, soft[:, :BLOCK], 0.0)
                if end < rows:
                    soft = jnp.concatenate([edge, soft[:, BLOCK:]], axis=1)
                else:
                    soft = edge
                grad = dot_nt(vh[first:end], g_low[first:])
                grad = (soft * (grad - delta[:, first:])).astype(LOW)
                value_parts[head].append(dot(soft.astype(LOW), g_low[first:]))
                key_parts[head].append(dot(grad, q_low[first:]))
                added = dot_tn(grad, k_low[first:end])
                if first == 0:
                    sum_ref[head] = added
                else:
                    sum_ref[head, first:, :] += added
        lane_here = lane[:BLOCK]
        for step in range(rows // BLOCK):
            first, end = step * BLOCK, (step + 1) * BLOCK
            dk = jnp.where(lane_here < HEAD_DIM, key_parts[0][step], key_parts[1][step])
            dv = jnp.where(lane_here < HEAD_DIM, value_parts[0][step], value_parts[1][step])
            dq = jnp.where(lane_here < HEAD_DIM, sum_ref[0, first:end, :], sum_ref[1, first:end, :])
            dk_ref[first:end, :] = unrotate(dk, first, end).astype(LOW)
            dq_ref[first:end, :] = unrotate(dq * HEAD_DIM**-0.5, first, end).astype(LOW)
            dv_ref[first:end, :] = dv.astype(LOW)

    return call(
        kernel,
        at,
        [queries, key_rows, value_rows, mixed, logs, upstream, cosine, sine, *before],
        [pair_spec(rows, first_pair)] * 4
        + [logs_spec(rows, first_pair), pair_spec(rows, first_pair)]
        + [whole_spec((rows, PAIR))] * 2
        + [ANYWHERE] * len(before),
        [shape_of((rows, width), LOW)] * 3,
        [pair_spec(rows, first_pair)] * 3,
        [pltpu.VMEM((2, rows, PAIR), F32)],
        pairs,
        5 * pairs,
        {9 + i: i for i in range(len(before))},
    )


def open_block(at, mixed, resid, gain, pieces):
    rows, width = mixed.shape
    half = width // 2
    n = len(pieces)
    cols = weight_shape(pieces)[2]
    wide = (cols - half) // 2

    def kernel(at_ref, o_ref, resid_ref, gain_ref, *refs):
        parts, outs, (w_ref, sems) = refs[:n], refs[n : n + 5], refs[n + 5 :]
        r_ref, hl_ref, gate_ref, up_ref, z_ref = outs
        load_first(at_ref, (parts, w_ref, sems))
        o = o_ref[...]
        branch = jnp.concatenate([dot(o, w_ref[c, :, :half]) for c in range(2)], axis=1)
        r = resid_ref[...].astype(F32) + branch
        r_ref[...] = r
        hl = (r * inverse_rms(r) * gain_ref[...]).astype(LOW)
        hl_ref[...] = hl
        for c in range(2):
            gate = dot(hl, w_ref[c, :, half : half + wide])
            up = dot(hl, w_ref[c, :, half + wide :])
            here = slice(c * wide, (c + 1) * wide)
            gate_ref[:, here] = gate.astype(LOW)
            up_ref[:, here] = up.astype(LOW)
            z_ref[:, here] = (silu_parts(gate)[1] * up).astype(LOW)

    return call(
        kernel,
        at,
        [mixed, resid, gain, *pieces],
        [rows_spec(width), rows_spec(width), whole_spec((1, width))] + [ANYWHERE] * n,
        [shape_of((rows, width), F32), shape_of((rows, width), LOW)]
        + [shape_of((rows, 2 * wide), LOW)] * 3,
        [rows_spec(width)] * 2 + [rows_spec(2 * wide)] * 3,
        weight_scratch(pieces),
        rows // BLOCK,
        16,
    )


def close_first(at, hidden, resid, gains, pieces):
    rows, width = resid.shape
    wide = hidden.shape[1]
    n = len(pieces)

    def kernel(at_ref, z_ref, r_ref, gain_ref, *refs):
        parts, (r2_ref, out_ref, next_ref), (w_ref, sems) = refs[:n], refs[n : n + 3], refs[n + 3 :]
        load_first(at_ref, (parts, w_ref, sems))
        z = z_ref[...]
        r = r_ref[...]
        branch = jnp.concatenate([dot(z, w_ref[c]) for c in range(2)], axis=1)
        r2 = r * inverse_rms(r) * gain_ref[0:1] + branch
        r2_ref[...] = r2
        out = r2 * inverse_rms(r2) * gain_ref[1:2]
        out_ref[...] = out
        next_ref[...] = (out * inverse_rms(out) * gain_ref[2:3]).astype(LOW)

    return call(
        kernel,
        at,
        [hidden, resid, gains, *pieces],
        [rows_spec(wide), rows_spec(width), whole_spec(gains.shape)] + [ANYWHERE] * n,
        [shape_of((rows, width), F32)] * 2 + [shape_of((rows, width), LOW)],
        [rows_spec(width)] * 3,
        weight_scratch(pieces),
        rows // BLOCK,
        12,
    )


def close_second(at, hidden, resid, pieces):
    rows, width = resid.shape
    wide = hidden.shape[1]
    n = len(pieces)

    def kernel(at_ref, z_ref, r_ref, *refs):
        parts, out_ref, (w_ref, sems) = refs[:n], refs[n], refs[n + 1 :]
        load_first(at_ref, (parts, w_ref, sems))
        z = z_ref[...]
        branch = jnp.concatenate([dot(z, w_ref[c]) for c in range(2)], axis=1)
        out_ref[...] = r_ref[...] + branch

    return call(
        kernel,
        at,
        [hidden, resid, *pieces],
        [rows_spec(wide), rows_spec(width)] + [ANYWHERE] * n,
        shape_of((rows, width), F32),
        rows_spec(width),
        weight_scratch(pieces),
        rows // BLOCK,
        6,
    )


def feed_back(at, upstream, up_low, gate, up, resid, gain, pieces, down, post):
    rows, width = resid.shape
    half, wide = width // 2, gate.shape[1]
    part = wide // 2
    n, m = len(pieces), len(down)

    def kernel(at_ref, du_ref, dl_ref, gate_ref, up_ref, r_ref, gain_ref, *refs):
        parts, down_parts, refs = refs[:n], refs[n : n + m], refs[n + m :]
        dgate_ref, dup_ref, dr_ref, dlow_ref, do_ref, dgain_ref = refs[:6]
        w_ref, sems, d_ref, d_sems = refs[6:]
        load_first(at_ref, (parts, w_ref, sems), (down_parts, d_ref, d_sems))
        dl = dl_ref[...]
        inward = None
        for c in range(2):
            here = slice(c * part, (c + 1) * part)
            dz = dot_nt(dl[:, :half], d_ref[0, here, :]) + dot_nt(dl[:, half:], d_ref[1, here, :])
            gate = gate_ref[:, here].astype(F32)
            sig, act = silu_parts(gate)
            dup = (dz * act).astype(LOW)
            dgate = dz * up_ref[:, here].astype(F32) * sig * (1.0 + gate * (1.0 - sig))
            dgate = dgate.astype(LOW)
            dup_ref[:, here] = dup
            dgate_ref[:, here] = dgate
            added = dot_nt(dgate, w_ref[c, :, half : half + part])
            added = added + dot_nt(dup, w_ref[c, :, half + part :])
            inward = added if inward is None else inward + added
        du = du_ref[...].astype(F32)
        if post:
            dr, share = norm_back(r_ref[...], gain_ref[...], du + inward)
        else:
            dr, share = norm_back(r_ref[...], gain_ref[...], inward)
            dr = du + dr
        dr_ref[...] = dr
        low = dr.astype(LOW)
        dlow_ref[...] = low
        do = dot_nt(low[:, :half], w_ref[0, :, :half]) + dot_nt(low[:, half:], w_ref[1, :, :half])
        do_ref[...] = do.astype(LOW)

        @pl.when(pl.program_id(0) == 0)
        def _():
            dgain_ref[...] = jnp.zeros_like(dgain_ref)

        dgain_ref[...] += fold_rows(share)

    return call(
        kernel,
        at,
        [upstream, up_low, gate, up, resid, gain, *pieces, *down],
        [rows_spec(width)] * 2
        + [rows_spec(wide)] * 2
        + [rows_spec(width), whole_spec((1, width))]
        + [ANYWHERE] * (n + m),
        [shape_of((rows, wide), LOW)] * 2
        + [shape_of((rows, width), F32)]
        + [shape_of((rows, width), LOW)] * 2
        + [shape_of((8, width), F32)],
        [rows_spec(wide)] * 2 + [rows_spec(width)] * 3 + [whole_spec((8, width))],
        weight_scratch(pieces) + weight_scratch(down),
        rows // BLOCK,
        27,
    )


def heads_inward(dq, dk, dv, w_ref):
    half = dq.shape[1] // 2
    inward = None
    for c in range(2):
        here = slice(c * half, (c + 1) * half)
        joined = jnp.concatenate([dq[:, here], dk[:, here], dv[:, here]], axis=1)
        added = dot_nt(joined, w_ref[c])
        inward = added if inward is None else inward + added
    return inward


def heads_back_second(at, dq, dk, dv, upstream, first_out, resid_two, gains, pieces):
    rows, width = dq.shape
    n = len(pieces)

    def kernel(at_ref, dq_ref, dk_ref, dv_ref, du_ref, h_ref, r_ref, gain_ref, *refs):
        parts, refs = refs[:n], refs[n:]
        dr_ref, dlow_ref, ga_ref, gb_ref, w_ref, sems = refs
        load_first(at_ref, (parts, w_ref, sems))
        inward = heads_inward(dq_ref[...], dk_ref[...], dv_ref[...], w_ref)
        back, share_a = norm_back(h_ref[...], gain_ref[0:1], inward)
        dr, share_b = norm_back(r_ref[...], gain_ref[1:2], du_ref[...] + back)
        dr_ref[...] = dr
        dlow_ref[...] = dr.astype(LOW)

        @pl.when(pl.program_id(0) == 0)
        def _():
            ga_ref[...] = jnp.zeros_like(ga_ref)
            gb_ref[...] = jnp.zeros_like(gb_ref)

        ga_ref[...] += fold_rows(share_a)
        gb_ref[...] += fold_rows(share_b)

    return call(
        kernel,
        at,
        [dq, dk, dv, upstream, first_out, resid_two, gains, *pieces],
        [rows_spec(width)] * 6 + [whole_spec(gains.shape)] + [ANYWHERE] * n,
        [shape_of((rows, width), F32), shape_of((rows, width), LOW)]
        + [shape_of((8, width), F32)] * 2,
        [rows_spec(width)] * 2 + [whole_spec((8, width))] * 2,
        weight_scratch(pieces),
        rows // BLOCK,
        14,
    )


def heads_back_first(at, dq, dk, dv, upstream, pieces):
    rows, width = dq.shape
    n = len(pieces)

    def kernel(at_ref, dq_ref, dk_ref, dv_ref, du_ref, *refs):
        parts, (out_ref, w_ref, sems) = refs[:n], refs[n:]
        load_first(at_ref, (parts, w_ref, sems))
        out_ref[...] = du_ref[...] + heads_inward(dq_ref[...], dk_ref[...], dv_ref[...], w_ref)

    return call(
        kernel,
        at,
        [dq, dk, dv, upstream, *pieces],
        [rows_spec(width)] * 4 + [ANYWHERE] * n,
        shape_of((rows, width), F32),
        rows_spec(width),
        weight_scratch(pieces),
        rows // BLOCK,
        8,
    )


def weight_grad(half, groups, received):
    rows = groups[0][0].shape[0]
    lefts = [left for left, _ in groups]
    rights = [right for _, many in groups for right in many]
    counts = [len(many) for _, many in groups]
    tall = lefts[0].shape[1]
    sizes = [right.shape[1] // 2 for right in rights]
    extra = [] if received is None else [received]

    def kernel(half_ref, *refs):
        left_refs, refs = refs[: len(lefts)], refs[len(lefts) :]
        right_refs, refs = refs[: len(rights)], refs[len(rights) :]
        out_ref = refs[-1]
        offset, at = 0, 0
        for left_ref, count in zip(left_refs, counts):
            left = left_ref[...]
            for right_ref in right_refs[at : at + count]:
                size = right_ref.shape[1]
                here = slice(offset, offset + size)
                res = dot_tn(left, right_ref[...])
                if extra:
                    res = res + refs[0][:, here].astype(F32)
                out_ref[:, here] = res.astype(LOW)
                offset += size
            at += count

    total = sum(sizes)
    return call(
        kernel,
        half,
        lefts + rights + extra,
        [whole_spec((rows, tall))] * len(lefts)
        + [pl.BlockSpec((rows, size), lambda i, at: (0, at[0])) for size in sizes]
        + [whole_spec((tall, total))] * len(extra),
        shape_of((tall, total), LOW),
        whole_spec((tall, total)),
        [],
        1,
        7,
    )


def tie(value, *others):
    others = [other for other in others if other is not None]
    return lax.optimization_barrier((value, *others))[0] if others else value


def place_of():
    f = lax.axis_index("fsdp")
    r = lax.axis_index("rep")
    return (f // 2, f % 2, r // 2, r % 2)


def shift_z(grid, k):
    return lambda z, y, x, c: ((z + k) % grid.zs, y, x, c)


def pick(array, index, axis):
    return lax.dynamic_index_in_dim(array, index, axis, keepdims=False)


def add_low(one, two):
    return (one.astype(F32) + two.astype(F32)).astype(LOW)


def join_halves(left, right, widths):
    out, offset = [], 0
    for width in widths:
        here = slice(offset, offset + width // 2)
        out.append(jnp.concatenate([left[:, here], right[:, here]], axis=1))
        offset += width // 2
    return out


class Gather:
    def __init__(self, link, shards, after=None):
        z, y, x, c = link.place
        grid = self.grid = link.grid
        rows = shards[0].shape[0] // 2
        own = jnp.concatenate(
            [
                lax.dynamic_slice(
                    shard, (x * rows, c * (shard.shape[1] // 2)), (rows, shard.shape[1] // 2)
                )
                for shard in shards
            ],
            axis=1,
        )
        own = tie(own, after)
        around = [own] + [send(grid, own, shift_z(grid, k)) for k in range(1, grid.zs)]
        self.base = jnp.stack(around)

    def near(self, *after):
        base = tie(self.base, *after)
        self.one = send(self.grid, base, first_flip)
        self.two = send(self.grid, base, second_flip)
        return self.one

    def far(self, *after):
        self.three = send(self.grid, tie(self.one, *after), second_flip)
        return self.three

    def whole(self, *after):
        near = [self.base, self.one, self.two, self.three]
        return near + [send(self.grid, part, core_flip) for part in near]


class PlainGather:
    base = one = three = None

    def __init__(self, link, shards, after=None):
        self.shards = shards

    def near(self, *after):
        return None

    def far(self, *after):
        return None

    def whole(self, *after):
        full = [lax.all_gather(shard, "fsdp", axis=0, tiled=True) for shard in self.shards]
        halves = [
            jnp.concatenate([jnp.split(weight, 2, axis=1)[c] for weight in full], axis=1)
            for c in range(2)
        ]
        return [jnp.stack(halves)]


class Reduce:
    def __init__(self, link, make, widths, *after):
        self.link, self.make, self.widths = link, make, widths
        self.away = make(tie(link.other, *after), None)
        self.got = send(link.grid, self.away, core_flip)

    def mine(self, *after):
        z, y, x, c = self.link.place
        half = self.make(tie(self.link.mine, *after), self.got)
        zs = self.link.grid.zs
        rows, cols = half.shape[0] // (4 * zs), half.shape[1]
        view = half.reshape(zs, 2, 2, rows, cols)
        self.keep = jnp.where(c == 0, pick(view, y, 1), pick(view, x, 2))
        away = jnp.where(c == 0, pick(view, 1 - y, 1), pick(view, 1 - x, 2))
        self.got = send(self.link.grid, away, second_flip)
        return half

    def one(self, *after):
        z, y, x, c = self.link.place
        part = add_low(self.keep, tie(self.got, *after))
        b = jnp.where(c == 0, x, y)
        self.keep = pick(part, b, 1)
        away = pick(part, 1 - b, 1)
        self.got = send(self.link.grid, away, first_flip)
        return away

    def two(self, *after):
        grid = self.link.grid
        z = self.link.place[0]
        part = add_low(self.keep, tie(self.got, *after))
        self.keep = pick(part, z, 0)
        self.got = [
            send(grid, pick(part, (z + k) % grid.zs, 0), shift_z(grid, k))
            for k in range(1, grid.zs)
        ]
        return part

    def three(self, *after):
        total = tie(self.keep, *after).astype(F32)
        for got in self.got:
            total = total + got.astype(F32)
        self.keep = total.astype(LOW)
        self.got = send(self.link.grid, self.keep, x_flip)
        return self.keep

    def four(self, *after):
        x = self.link.place[2]
        self.got = tie(self.got, *after)
        self.keep = jnp.concatenate(
            [jnp.where(x == 0, self.keep, self.got), jnp.where(x == 0, self.got, self.keep)],
            axis=0,
        )
        self.got = send(self.link.grid, self.keep, core_flip)
        return self.keep

    def out(self, *after):
        c = self.link.place[3]
        self.got = tie(self.got, *after)
        left = jnp.where(c == 0, self.keep, self.got).astype(F32)
        right = jnp.where(c == 0, self.got, self.keep).astype(F32)
        return join_halves(left, right, self.widths)


class PlainReduce:
    away = None

    def __init__(self, link, make, widths, *after):
        self.make, self.widths = make, widths

    def mine(self, *after):
        return None

    one = two = three = four = mine

    def out(self, *after):
        halves = [self.make(jnp.full((1,), c, jnp.int32), None) for c in range(2)]
        share = lax.psum_scatter(
            jnp.stack(halves, axis=1), "fsdp", scatter_dimension=0, tiled=True
        )
        share = lax.psum(share, "rep").astype(F32)
        return join_halves(share[:, 0], share[:, 1], self.widths)


class Direct:
    gather, reduce = Gather, Reduce

    def __init__(self, fsdp, rep):
        self.grid = Grid(fsdp, rep)
        self.place = place_of()
        self.at = jnp.stack(self.place).astype(jnp.int32)
        self.mine = self.at[3:4]
        self.other = 1 - self.mine

    def gains(self, own):
        z, y, x, c = self.place
        grid = self.grid
        around = [own] + [send(grid, own, shift_z(grid, k)) for k in range(1, grid.zs)]
        base = jnp.stack(around)
        both = jnp.stack([base, send(grid, base, y_flip)])
        blocks = []
        for zz in range(grid.zs):
            level = pick(both, (z + grid.zs - zz) % grid.zs, 1)
            for yy in range(2):
                blocks.append(pick(level, jnp.abs(y - yy), 0))
        return jnp.concatenate(blocks, axis=1)

    def reduce_gains(self, value):
        z, y, x, c = self.place
        grid = self.grid
        for flip in (core_flip, x_flip, y_flip):
            value = value + send(grid, value, flip)
        total = value
        for k in range(1, grid.zs):
            total = total + send(grid, value, shift_z(grid, k))
        share = total.shape[1] // (2 * grid.zs)
        return lax.dynamic_slice_in_dim(total, (z * 2 + y) * share, share, 1)


class Plain:
    gather, reduce = PlainGather, PlainReduce

    def __init__(self):
        self.at = jnp.zeros((4,), jnp.int32)

    def gains(self, own):
        return lax.all_gather(own, "fsdp", axis=1, tiled=True)

    def reduce_gains(self, value):
        share = lax.psum_scatter(value, "fsdp", scatter_dimension=1, tiled=True)
        return lax.psum(share, "rep")


def rope_tables(positions):
    even_steps = jnp.arange(0, HEAD_DIM, 2).astype(F32)
    inverse = jnp.exp(even_steps * (-math.log(10000.0) / HEAD_DIM))
    angles = positions.astype(F32)[:, None] * inverse
    cosine, sine = jnp.cos(angles), jnp.sin(angles)
    return jnp.concatenate([cosine] * 4, axis=1), jnp.concatenate([-sine, sine] * 2, axis=1)


def body(
    fsdp,
    rep,
    tokens,
    cotangent,
    seq_lengths,
    token_positions,
    first_query,
    first_key,
    first_value,
    first_output,
    first_gate,
    first_up,
    first_down,
    first_attngain,
    first_ffngain,
    second_query,
    second_key,
    second_value,
    second_output,
    second_gate,
    second_up,
    second_down,
    second_attngain,
    second_ffngain,
):
    _, rows, width = tokens.shape
    wide = first_gate.shape[1]
    low_tokens = tokens.reshape(rows, width)
    low_cot = cotangent.reshape(rows, width)
    link = Direct(fsdp, rep) if (fsdp, rep) == (8, 4) else Plain()
    at = jnp.concatenate([link.at, seq_lengths.astype(jnp.int32)])
    cosine, sine = rope_tables(token_positions.reshape(rows))
    pairs = width // PAIR
    split = pairs // 2
    attn_widths, open_widths = (width,) * 3, (width, wide, wide)

    heads_one = link.gather(link, (first_query, first_key, first_value))
    gains = link.gains(
        jnp.stack([first_attngain, first_ffngain, second_attngain, second_ffngain])
    ).astype(F32)
    attn_one, ffn_one, attn_two, ffn_two = (gains[i : i + 1] for i in range(4))
    open_one = link.gather(link, (first_output, first_gate, first_up), heads_one.base)
    heads_one.near()
    far = heads_one.far()
    down_one = link.gather(link, (first_down,), open_one.base)
    open_one.near(far)
    heads_one = heads_one.whole()
    q1, k1, v1 = project_heads(at, low_tokens, heads_one, cosine, sine)
    half = attend(at, tie(q1, down_one.base), k1, v1, 0, split)
    open_one.far()
    heads_two = link.gather(link, (second_query, second_key, second_value), down_one.base)
    o1, log1 = attend(at, tie(q1, open_one.one), k1, v1, split, pairs - split, half)
    down_one.near(open_one.three)
    open_one = open_one.whole()
    r1, h1, gate1, up1, z1 = open_block(at, o1, low_tokens, attn_one, open_one)
    far = down_one.far()
    heads_two.near(far)
    open_two = link.gather(link, (second_output, second_gate, second_up), heads_two.base)
    down_one = down_one.whole()
    r2, first_out, n1 = close_first(at, z1, r1, gains, down_one)
    far = heads_two.far()
    heads_two = heads_two.whole()
    q2, k2, v2 = project_heads(at, n1, heads_two, cosine, sine)
    open_two.near(far)
    down_two = link.gather(link, (second_down,), open_two.base)
    half = attend(at, q2, k2, v2, 0, split)
    open_two.far()
    o2, log2 = attend(at, tie(q2, open_two.one), k2, v2, split, pairs - split, half)
    down_two.near(open_two.three)
    open_two = open_two.whole()
    r3, h2, gate2, up2, z2 = open_block(at, o2, first_out, ffn_two, open_two)
    down_two.far()
    down_two = down_two.whole()
    second_out = close_second(at, z2, r3, down_two)

    dgate2, dup2, dr3, dr3_low, do2, gain_d = feed_back(
        at, low_cot, low_cot, gate2, up2, r3, ffn_two, open_two, down_two, False
    )
    down_g2 = link.reduce(
        link, lambda half, got: weight_grad(half, [(z2, [low_cot])], got), (width,), dr3
    )
    open_g2 = link.reduce(
        link,
        lambda half, got: weight_grad(half, [(o2, [dr3_low]), (h2, [dgate2, dup2])], got),
        open_widths,
        down_g2.away,
    )
    sent = down_g2.mine(open_g2.away)
    sent = open_g2.mine(sent)
    half = attend_back(at, tie(q2, sent), k2, v2, o2, log2, do2, cosine, sine, 0, split)
    part = down_g2.one(half[0])
    dq2, dk2, dv2 = attend_back(
        at, tie(q2, part), k2, v2, o2, log2, do2, cosine, sine, split, pairs - split, half
    )
    part = (open_g2.one(dq2), down_g2.two(dq2))
    heads_g2 = link.reduce(
        link, lambda half, got: weight_grad(half, [(n1, [dq2, dk2, dv2])], got), attn_widths, *part
    )
    dr2, dr2_low, gain_c, gain_b = heads_back_second(
        tie(at, heads_g2.away),
        dq2,
        dk2,
        dv2,
        dr3,
        first_out,
        r2,
        jnp.concatenate([attn_two, ffn_one]),
        heads_two,
    )
    part = (open_g2.two(dr2), down_g2.three(dr2))
    sent = heads_g2.mine(dr2, *part)

    dgate1, dup1, dr1, dr1_low, do1, gain_a = feed_back(
        tie(at, sent), dr2, dr2_low, gate1, up1, r1, attn_one, open_one, down_one, True
    )
    part = (open_g2.three(dr1), heads_g2.one(dr1), down_g2.four(dr1))
    down_g1 = link.reduce(
        link, lambda half, got: weight_grad(half, [(z1, [dr2_low])], got), (width,), dr1, *part
    )
    open_g1 = link.reduce(
        link,
        lambda half, got: weight_grad(half, [(o1, [dr1_low]), (h1, [dgate1, dup1])], got),
        open_widths,
        down_g1.away,
    )
    part = (heads_g2.two(open_g1.away), open_g2.four(open_g1.away))
    sent = down_g1.mine(open_g1.away, *part)
    sent = open_g1.mine(sent)
    gain_grads = link.reduce_gains(
        jnp.stack([jnp.sum(share, axis=0) for share in (gain_a, gain_b, gain_c, gain_d)])
    )
    half = attend_back(at, tie(q1, sent), k1, v1, o1, log1, do1, cosine, sine, 0, split)
    part = (down_g1.one(half[0]), heads_g2.three(half[0]))
    dq1, dk1, dv1 = attend_back(
        at, tie(q1, *part), k1, v1, o1, log1, do1, cosine, sine, split, pairs - split, half
    )
    part = (open_g1.one(dq1), down_g1.two(dq1), heads_g2.four(dq1))
    heads_g1 = link.reduce(
        link,
        lambda half, got: weight_grad(half, [(low_tokens, [dq1, dk1, dv1])], got),
        attn_widths,
        *part,
    )
    part = (open_g1.two(heads_g1.away), down_g1.three(heads_g1.away))
    sent = heads_g1.mine(*part)
    input_grad = heads_back_first(tie(at, sent), dq1, dk1, dv1, dr1, heads_one)
    part = heads_g1.one(input_grad)
    down_g1.four(input_grad)
    part = heads_g1.two()
    open_g1.three(part)
    down_g1 = down_g1.out(part)
    output_g2, gate_g2, up_g2 = open_g2.out(part)
    query_g2, key_g2, value_g2 = heads_g2.out(part)
    (down_g2,) = down_g2.out(part)
    part = heads_g1.three()
    open_g1.four(part)
    (down_g1,) = down_g1
    heads_g1.four()
    query_g1, key_g1, value_g1 = heads_g1.out()
    output_g1, gate_g1, up_g1 = open_g1.out()
    return (
        first_out.reshape(tokens.shape),
        second_out.reshape(tokens.shape),
        input_grad.reshape(tokens.shape),
        query_g1,
        key_g1,
        value_g1,
        output_g1,
        gate_g1,
        up_g1,
        down_g1,
        gain_grads[0],
        gain_grads[1],
        query_g2,
        key_g2,
        value_g2,
        output_g2,
        gate_g2,
        up_g2,
        down_g2,
        gain_grads[2],
        gain_grads[3],
    )


def solution(mesh):
    per_seq = P(("fsdp", "rep"))
    shard = P("fsdp")
    return jax.shard_map(
        functools.partial(body, mesh.shape["fsdp"], mesh.shape["rep"]),
        mesh=mesh,
        in_specs=(per_seq,) * 4 + (shard,) * 18,
        out_specs=(per_seq,) * 3 + (shard,) * 18,
        check_vma=False,
    )
```

```python
import functools
import math

import jax
import jax.numpy as jnp
from jax import lax
from jax.experimental import pallas as pl
from jax.experimental.pallas import tpu as pltpu
from jax.sharding import PartitionSpec as P

HEAD_DIM = 64

epsilon = 1e-06
masked_score = -1e30


class Grid:
    def __init__(self, fsdp, rep):
        self.zs = fsdp // 2
        self.rep = rep

    def flat(self, z, y, x, c):
        return (z * 2 + y) * self.rep + x * 2 + c

    def pairs(self, move):
        out = []
        for z in range(self.zs):
            for y in range(2):
                for x in range(2):
                    for c in range(2):
                        out.append((self.flat(z, y, x, c), self.flat(*move(z, y, x, c))))
        return out


AXES = ("fsdp", "rep")


def send(grid, value, move):
    return lax.ppermute(value, AXES, grid.pairs(move))


def first_flip(z, y, x, c):
    return (z, y, 1 - x, c) if c == 0 else (z, 1 - y, x, c)


def second_flip(z, y, x, c):
    return (z, 1 - y, x, c) if c == 0 else (z, y, 1 - x, c)


def core_flip(z, y, x, c):
    return (z, y, x, 1 - c)


def x_flip(z, y, x, c):
    return (z, y, 1 - x, c)


def y_flip(z, y, x, c):
    return (z, 1 - y, x, c)

BLOCK = 256
PAIR = 2 * HEAD_DIM
VMEM = 32 * 1024 * 1024
F32 = jnp.float32
LOW = jnp.bfloat16


def dot(one, two):
    return jnp.dot(one, two, preferred_element_type=F32)


def dot_nt(one, two):
    return lax.dot_general(one, two, (((1,), (1,)), ((), ())), preferred_element_type=F32)


def dot_tn(one, two):
    return lax.dot_general(one, two, (((0,), (0,)), ((), ())), preferred_element_type=F32)


def inverse_rms(values):
    return lax.rsqrt(jnp.mean(values * values, axis=-1, keepdims=True) + epsilon)


def norm_back(values, scales, upstream):
    inv = inverse_rms(values)
    weighted = upstream * scales
    inner = jnp.mean(weighted * values, axis=-1, keepdims=True)
    return inv * weighted - values * (inv * inv * inv) * inner, upstream * values * inv


def fold_rows(values):
    return jnp.sum(values.reshape(values.shape[0] // 8, 8, values.shape[1]), axis=0)


def silu_parts(gate):
    sig = 0.5 * jnp.tanh(0.5 * gate) + 0.5
    return sig, gate * sig


def piece_place(at_ref, which, k):
    z, y, x, c = at_ref[0], at_ref[1], at_ref[2], at_ref[3]
    cc = c if which < 4 else 1 - c
    first, second = which % 2, (which % 4) // 2
    flip_x = jnp.where(cc == 0, first, second)
    flip_y = jnp.where(cc == 0, second, first)
    return jnp.bitwise_xor(z, k) * 2 + jnp.where(flip_y == 1, 1 - y, y), jnp.where(flip_x == 1, 1 - x, x), cc


def slabs(at_ref, pieces):
    count, rows, _ = pieces[0].shape
    if len(pieces) == 1:
        return [(pieces[0].at[i], i // 2 * rows, i % 2) for i in range(count)], rows
    out = []
    for which in range(8):
        for k in range(count):
            shard, x, c = piece_place(at_ref, which, k)
            row = pl.multiple_of(shard * (2 * rows) + x * rows, 16)
            out.append((pieces[which].at[k], row, c))
    return out, rows


def weight_copies(at_ref, pieces, w_refs, sems):
    copies = []
    places, rows = slabs(at_ref, pieces)
    for slab, row, c in places:
        offset = 0
        for w_ref in w_refs:
            half = w_ref.shape[1] // 2
            col = c * half if isinstance(c, int) else pl.multiple_of(c * half, 128)
            copies.append(
                pltpu.make_async_copy(
                    slab.at[:, pl.ds(offset, half)],
                    w_ref.at[pl.ds(row, rows), pl.ds(col, half)],
                    sems.at[len(copies)],
                )
            )
            offset += half
    return copies


def weight_scratch(pieces, widths):
    count, rows, _ = pieces[0].shape
    tall = count * rows // 2 if len(pieces) == 1 else count * 4 * rows
    copies = len(pieces) * count * len(widths)
    return [pltpu.VMEM((tall, width), LOW) for width in widths] + [
        pltpu.SemaphoreType.DMA((copies,))
    ]


def start_all(copies):
    for copy in copies:
        copy.start()
    return copies


def wait_all(copies):
    for copy in copies:
        copy.wait()


ANYWHERE = pl.BlockSpec(memory_space=pl.ANY)
HELD = pl.BlockSpec(memory_space=pltpu.HBM)
NEAR = pl.BlockSpec(memory_space=pltpu.VMEM)
SCALARS = pl.BlockSpec(memory_space=pltpu.SMEM)
MIB = 1024 * 1024


def cost(micros):
    return pl.CostEstimate(
        flops=int(micros * 1.1e9), bytes_accessed=int(micros * 1e5), transcendentals=0
    )


def call(kernel, at, near, weights, outs, scratch, micros, room):
    weights = [pltpu.with_memory_space_constraint(weight, pltpu.HBM) for weight in weights]
    return pl.pallas_call(
        kernel,
        out_shape=outs,
        in_specs=[SCALARS] + [NEAR] * len(near) + [HELD] * len(weights),
        out_specs=jax.tree.map(lambda _: NEAR, outs),
        scratch_shapes=scratch,
        compiler_params=pltpu.CompilerParams(vmem_limit_bytes=room * MIB),
        cost_estimate=cost(micros),
    )(at, *near, *weights)


def shape_of(shape, dtype):
    return jax.ShapeDtypeStruct(shape, dtype)


def blocks(rows):
    return [slice(first, first + BLOCK) for first in range(0, rows, BLOCK)]


def pair_spec(rows, first_pair):
    return pl.BlockSpec((rows, PAIR), lambda p, at: (0, p + first_pair))


def logs_spec(rows, first_pair):
    return pl.BlockSpec((1, 16, rows), lambda p, at: (p + first_pair, 0, 0))


def whole_spec(shape):
    return pl.BlockSpec(shape, lambda i, at: (0,) * len(shape))


def call_pairs(kernel, at, arrays, specs, outs, out_specs, scratch, steps, micros, aliases):
    arrays = [pltpu.with_memory_space_constraint(array, pltpu.HBM) for array in arrays]
    outs = [pltpu.HBM(out.shape, out.dtype) for out in outs]
    return pl.pallas_call(
        kernel,
        out_shape=outs,
        grid_spec=pltpu.PrefetchScalarGridSpec(
            num_scalar_prefetch=1,
            grid=(steps,),
            in_specs=specs,
            out_specs=out_specs,
            scratch_shapes=scratch,
        ),
        input_output_aliases=aliases,
        compiler_params=pltpu.CompilerParams(vmem_limit_bytes=16 * MIB),
        cost_estimate=cost(micros),
    )(at, *arrays)


def turn_lanes(values, lane):
    return jnp.where(
        (lane & (HEAD_DIM - 1)) < HEAD_DIM // 2,
        pltpu.roll(values, PAIR - HEAD_DIM // 2, 1),
        pltpu.roll(values, HEAD_DIM // 2, 1),
    )


def project_heads(at, inputs, pieces, cosine, sine):
    rows, width = inputs.shape
    n = len(pieces)

    def kernel(at_ref, a_ref, cos_ref, sin_ref, *refs):
        parts, (q_ref, k_ref, v_ref), (*w_refs, sems) = refs[:n], refs[n : n + 3], refs[n + 3 :]
        wait_all(start_all(weight_copies(at_ref, parts, w_refs, sems)))
        lane = lax.broadcasted_iota(jnp.int32, (BLOCK, PAIR), 1)
        for block in blocks(rows):
            a = a_ref[block, :]
            cos, sin = cos_ref[block, :], sin_ref[block, :]
            for first in range(0, width, 2 * PAIR):
                q = dot(a, w_refs[0][:, first : first + 2 * PAIR])
                k = dot(a, w_refs[1][:, first : first + 2 * PAIR])
                v = dot(a, w_refs[2][:, first : first + 2 * PAIR])
                for t in range(2):
                    here = slice(first + t * PAIR, first + (t + 1) * PAIR)
                    q_pair = q[:, t * PAIR : (t + 1) * PAIR]
                    k_pair = k[:, t * PAIR : (t + 1) * PAIR]
                    q_pair = q_pair * cos + turn_lanes(q_pair, lane) * sin
                    q_ref[block, here] = (q_pair * HEAD_DIM**-0.5).astype(LOW)
                    k_ref[block, here] = (k_pair * cos + turn_lanes(k_pair, lane) * sin).astype(LOW)
                v_ref[block, first : first + 2 * PAIR] = v.astype(LOW)

    return call(
        kernel,
        at,
        [inputs, cosine, sine],
        pieces,
        [shape_of((rows, width), LOW)] * 3,
        weight_scratch(pieces, (width,) * 3),
        8,
        16,
    )


def head_masks(head, lane):
    own = lane < HEAD_DIM if head == 0 else lane >= HEAD_DIM
    return own, lane == (HEAD_DIM if head == 0 else 0)


def attend(at, queries, key_rows, value_rows, first_pair, pairs, before=()):
    rows, width = queries.shape
    every = width // PAIR

    def kernel(at_ref, q_ref, k_ref, v_ref, *refs):
        o_ref, lse_ref = refs[len(before) :]
        lane = lax.broadcasted_iota(jnp.int32, (rows, PAIR), 1)
        row = lax.broadcasted_iota(jnp.int32, (rows, PAIR), 0)
        bias = jnp.where(row < at_ref[4], 0.0, masked_score)
        q, k, v = q_ref[...].astype(F32), k_ref[...].astype(F32), v_ref[...].astype(F32)
        below = lax.broadcasted_iota(jnp.int32, (BLOCK, BLOCK), 0) >= lax.broadcasted_iota(
            jnp.int32, (BLOCK, BLOCK), 1
        )
        heads = []
        for head in range(2):
            own, mark = head_masks(head, lane)
            heads.append(
                (
                    jnp.where(own, q, jnp.where(mark, 1.0, 0.0)).astype(LOW),
                    jnp.where(own, k, jnp.where(mark, bias, 0.0)).astype(LOW),
                    jnp.where(own, v, 1.0).astype(LOW),
                )
            )
        lane_here = lane[:BLOCK]
        for first in range(0, rows, BLOCK):
            end = first + BLOCK
            mixed, logs = [], []
            for qh, kh, vh in heads:
                scores = [
                    dot_nt(qh[first:end], kh[start : start + BLOCK]) for start in range(0, end, BLOCK)
                ]
                scores[-1] = jnp.where(below, scores[-1], masked_score)
                top = functools.reduce(jnp.maximum, scores)
                top = jnp.max(top, axis=-1, keepdims=True)
                weights = [jnp.exp(part - top).astype(LOW) for part in scores]
                weights = jnp.concatenate(weights, axis=1) if first else weights[0]
                both = dot(weights, vh[:end])
                total = pltpu.roll(both, HEAD_DIM, 1)
                mixed.append(both / total)
                logs.append(top + jnp.log(total))
            o_ref[first:end, :] = jnp.where(lane_here < HEAD_DIM, mixed[0], mixed[1]).astype(LOW)
            turned = jnp.where(lane_here < HEAD_DIM, logs[0], logs[1]).T
            lse_ref[0, 0:8, first:end] = turned[0:8]
            lse_ref[0, 8:16, first:end] = turned[HEAD_DIM : HEAD_DIM + 8]

    return call_pairs(
        kernel,
        at,
        [queries, key_rows, value_rows, *before],
        [pair_spec(rows, first_pair)] * 3 + [ANYWHERE] * len(before),
        [shape_of((rows, width), LOW), shape_of((every, 16, rows), F32)],
        [pair_spec(rows, first_pair), logs_spec(rows, first_pair)],
        [],
        pairs,
        4 * pairs,
        {4 + i: i for i in range(len(before))},
    )


def attend_back(
    at, queries, key_rows, value_rows, mixed, logs, upstream, cosine, sine, first_pair, pairs, before=()
):
    rows, width = queries.shape

    def kernel(at_ref, q_ref, k_ref, v_ref, o_ref, lse_ref, g_ref, cos_ref, sin_ref, *refs):
        dq_ref, dk_ref, dv_ref, sum_ref = refs[len(before) :]
        lane = lax.broadcasted_iota(jnp.int32, (rows, PAIR), 1)
        row = lax.broadcasted_iota(jnp.int32, (rows, PAIR), 0)
        bias = jnp.where(row < at_ref[4], 0.0, masked_score)
        q, k, v = q_ref[...].astype(F32), k_ref[...].astype(F32), v_ref[...].astype(F32)
        q_low, k_low, g_low = q_ref[...], k_ref[...], g_ref[...]
        above = lax.broadcasted_iota(jnp.int32, (BLOCK, BLOCK), 0) <= lax.broadcasted_iota(
            jnp.int32, (BLOCK, BLOCK), 1
        )
        turned = (g_low.astype(F32) * o_ref[...].astype(F32)).T
        cos, sin = cos_ref[...], sin_ref[...]

        def unrotate(values, first, end):
            moved = values * sin[first:end]
            return values * cos[first:end] + turn_lanes(moved, lane[first:end])

        key_parts, value_parts = [], []
        for head in range(2):
            own, mark = head_masks(head, lane)
            qh = jnp.where(own, q, jnp.where(mark, 1.0, 0.0)).astype(LOW)
            kh = jnp.where(own, k, jnp.where(mark, bias, 0.0)).astype(LOW)
            vh = jnp.where(own, v, 0.0).astype(LOW)
            delta = jnp.sum(
                turned[head * HEAD_DIM : (head + 1) * HEAD_DIM], axis=0, keepdims=True
            )
            lse = lse_ref[0, head * 8 : head * 8 + 1, :]
            key_parts.append([])
            value_parts.append([])
            for first in range(0, rows, BLOCK):
                end = first + BLOCK
                scores = dot_nt(kh[first:end], qh[first:])
                soft = jnp.exp(scores - lse[:, first:])
                edge = jnp.where(above, soft[:, :BLOCK], 0.0)
                if end < rows:
                    soft = jnp.concatenate([edge, soft[:, BLOCK:]], axis=1)
                else:
                    soft = edge
                grad = dot_nt(vh[first:end], g_low[first:])
                grad = (soft * (grad - delta[:, first:])).astype(LOW)
                value_parts[head].append(dot(soft.astype(LOW), g_low[first:]))
                key_parts[head].append(dot(grad, q_low[first:]))
                added = dot_tn(grad, k_low[first:end])
                if first == 0:
                    sum_ref[head] = added
                else:
                    sum_ref[head, first:, :] += added
        lane_here = lane[:BLOCK]
        for step in range(rows // BLOCK):
            first, end = step * BLOCK, (step + 1) * BLOCK
            dk = jnp.where(lane_here < HEAD_DIM, key_parts[0][step], key_parts[1][step])
            dv = jnp.where(lane_here < HEAD_DIM, value_parts[0][step], value_parts[1][step])
            dq = jnp.where(lane_here < HEAD_DIM, sum_ref[0, first:end, :], sum_ref[1, first:end, :])
            dk_ref[first:end, :] = unrotate(dk, first, end).astype(LOW)
            dq_ref[first:end, :] = unrotate(dq * HEAD_DIM**-0.5, first, end).astype(LOW)
            dv_ref[first:end, :] = dv.astype(LOW)

    return call_pairs(
        kernel,
        at,
        [queries, key_rows, value_rows, mixed, logs, upstream, cosine, sine, *before],
        [pair_spec(rows, first_pair)] * 4
        + [logs_spec(rows, first_pair), pair_spec(rows, first_pair)]
        + [whole_spec((rows, PAIR))] * 2
        + [ANYWHERE] * len(before),
        [shape_of((rows, width), LOW)] * 3,
        [pair_spec(rows, first_pair)] * 3,
        [pltpu.VMEM((2, rows, PAIR), F32)],
        pairs,
        5 * pairs,
        {9 + i: i for i in range(len(before))},
    )


def open_block(at, mixed, resid, gain, pieces, wide):
    rows, width = mixed.shape
    n = len(pieces)

    def kernel(at_ref, o_ref, resid_ref, gain_ref, *refs):
        parts, outs, (*w_refs, sems) = refs[:n], refs[n : n + 5], refs[n + 5 :]
        r_ref, hl_ref, gate_ref, up_ref, z_ref = outs
        wait_all(start_all(weight_copies(at_ref, parts, w_refs, sems)))
        for block in blocks(rows):
            r = resid_ref[block, :].astype(F32) + dot(o_ref[block, :], w_refs[0][...])
            r_ref[block, :] = r
            hl = (r * inverse_rms(r) * gain_ref[...]).astype(LOW)
            hl_ref[block, :] = hl
            for first in range(0, wide, BLOCK):
                here = slice(first, first + BLOCK)
                gate = dot(hl, w_refs[1][:, here])
                up = dot(hl, w_refs[2][:, here])
                gate_ref[block, here] = gate.astype(LOW)
                up_ref[block, here] = up.astype(LOW)
                z_ref[block, here] = (silu_parts(gate)[1] * up).astype(LOW)

    return call(
        kernel,
        at,
        [mixed, resid, gain],
        pieces,
        [shape_of((rows, width), F32), shape_of((rows, width), LOW)]
        + [shape_of((rows, wide), LOW)] * 3,
        weight_scratch(pieces, (width, wide, wide)),
        12,
        20,
    )


def close_first(at, hidden, resid, gains, pieces):
    rows, width = resid.shape
    n = len(pieces)

    def kernel(at_ref, z_ref, r_ref, gain_ref, *refs):
        parts, (r2_ref, out_ref, next_ref), (w_ref, sems) = refs[:n], refs[n : n + 3], refs[n + 3 :]
        wait_all(start_all(weight_copies(at_ref, parts, [w_ref], sems)))
        for block in blocks(rows):
            r = r_ref[block, :]
            r2 = r * inverse_rms(r) * gain_ref[0:1] + dot(z_ref[block, :], w_ref[...])
            r2_ref[block, :] = r2
            out = r2 * inverse_rms(r2) * gain_ref[1:2]
            out_ref[block, :] = out
            next_ref[block, :] = (out * inverse_rms(out) * gain_ref[2:3]).astype(LOW)

    return call(
        kernel,
        at,
        [hidden, resid, gains],
        pieces,
        [shape_of((rows, width), F32)] * 2 + [shape_of((rows, width), LOW)],
        weight_scratch(pieces, (width,)),
        8,
        16,
    )


def close_second(at, hidden, resid, pieces):
    rows, width = resid.shape
    n = len(pieces)

    def kernel(at_ref, z_ref, r_ref, *refs):
        parts, out_ref, (w_ref, sems) = refs[:n], refs[n], refs[n + 1 :]
        wait_all(start_all(weight_copies(at_ref, parts, [w_ref], sems)))
        for block in blocks(rows):
            out_ref[block, :] = r_ref[block, :] + dot(z_ref[block, :], w_ref[...])

    return call(
        kernel,
        at,
        [hidden, resid],
        pieces,
        shape_of((rows, width), F32),
        weight_scratch(pieces, (width,)),
        7,
        16,
    )


def feed_back(at, upstream, up_low, gate, up, resid, gain, pieces, down, post):
    rows, width = resid.shape
    wide = gate.shape[1]
    n, m = len(pieces), len(down)

    def kernel(at_ref, du_ref, dl_ref, gate_ref, up_ref, r_ref, gain_ref, *refs):
        parts, down_parts, refs = refs[:n], refs[n : n + m], refs[n + m :]
        dgate_ref, dup_ref, dr_ref, dlow_ref, do_ref, dgain_ref = refs[:6]
        *w_refs, sems, d_ref, d_sems = refs[6:]
        down_copies = start_all(weight_copies(at_ref, down_parts, [d_ref], d_sems))
        copies = start_all(weight_copies(at_ref, parts, w_refs, sems))
        wait_all(down_copies)
        for block in blocks(rows):
            dl = dl_ref[block, :]
            for first in range(0, wide, BLOCK):
                here = slice(first, first + BLOCK)
                dz = dot_nt(dl, d_ref[here, :])
                gate = gate_ref[block, here].astype(F32)
                sig, act = silu_parts(gate)
                dup_ref[block, here] = (dz * act).astype(LOW)
                dgate = dz * up_ref[block, here].astype(F32) * (sig + act * (1.0 - sig))
                dgate_ref[block, here] = dgate.astype(LOW)
        wait_all(copies)
        shares = None
        for block in blocks(rows):
            inward = dot_nt(dgate_ref[block, :], w_refs[1][...])
            inward = inward + dot_nt(dup_ref[block, :], w_refs[2][...])
            du = du_ref[block, :].astype(F32)
            if post:
                dr, share = norm_back(r_ref[block, :], gain_ref[...], du + inward)
            else:
                dr, share = norm_back(r_ref[block, :], gain_ref[...], inward)
                dr = du + dr
            dr_ref[block, :] = dr
            low = dr.astype(LOW)
            dlow_ref[block, :] = low
            do_ref[block, :] = dot_nt(low, w_refs[0][...]).astype(LOW)
            share = fold_rows(share)
            shares = share if shares is None else shares + share
        dgain_ref[...] = shares

    return call(
        kernel,
        at,
        [upstream, up_low, gate, up, resid, gain],
        [*pieces, *down],
        [shape_of((rows, wide), LOW)] * 2
        + [shape_of((rows, width), F32)]
        + [shape_of((rows, width), LOW)] * 2
        + [shape_of((8, width), F32)],
        weight_scratch(pieces, (width, wide, wide)) + weight_scratch(down, (width,)),
        24,
        18,
    )


def heads_inward(block, grad_refs, w_refs):
    inward = dot_nt(grad_refs[0][block, :], w_refs[0][...])
    inward = inward + dot_nt(grad_refs[1][block, :], w_refs[1][...])
    return inward + dot_nt(grad_refs[2][block, :], w_refs[2][...])


def heads_back_second(at, dq, dk, dv, upstream, first_out, resid_two, gains, pieces):
    rows, width = dq.shape
    n = len(pieces)

    def kernel(at_ref, dq_ref, dk_ref, dv_ref, du_ref, h_ref, r_ref, gain_ref, *refs):
        parts, refs = refs[:n], refs[n:]
        dr_ref, dlow_ref, ga_ref, gb_ref, *w_refs, sems = refs
        wait_all(start_all(weight_copies(at_ref, parts, w_refs, sems)))
        sums = [None, None]
        for block in blocks(rows):
            inward = heads_inward(block, (dq_ref, dk_ref, dv_ref), w_refs)
            back, share_a = norm_back(h_ref[block, :], gain_ref[0:1], inward)
            dr, share_b = norm_back(r_ref[block, :], gain_ref[1:2], du_ref[block, :] + back)
            dr_ref[block, :] = dr
            dlow_ref[block, :] = dr.astype(LOW)
            for i, share in enumerate((share_a, share_b)):
                share = fold_rows(share)
                sums[i] = share if sums[i] is None else sums[i] + share
        ga_ref[...] = sums[0]
        gb_ref[...] = sums[1]

    return call(
        kernel,
        at,
        [dq, dk, dv, upstream, first_out, resid_two, gains],
        pieces,
        [shape_of((rows, width), F32), shape_of((rows, width), LOW)]
        + [shape_of((8, width), F32)] * 2,
        weight_scratch(pieces, (width,) * 3),
        8,
        16,
    )


def heads_back_first(at, dq, dk, dv, upstream, pieces):
    rows, width = dq.shape
    n = len(pieces)

    def kernel(at_ref, dq_ref, dk_ref, dv_ref, du_ref, *refs):
        parts, (out_ref, *w_refs, sems) = refs[:n], refs[n:]
        wait_all(start_all(weight_copies(at_ref, parts, w_refs, sems)))
        for block in blocks(rows):
            out_ref[block, :] = du_ref[block, :] + heads_inward(
                block, (dq_ref, dk_ref, dv_ref), w_refs
            )

    return call(
        kernel,
        at,
        [dq, dk, dv, upstream],
        pieces,
        shape_of((rows, width), F32),
        weight_scratch(pieces, (width,) * 3),
        7,
        16,
    )


def weight_grads(half, bundles, received):
    near, plan, outs = [], [], []
    for groups in bundles:
        total = 0
        for left, rights in groups:
            near.append(left)
            sizes = [right.shape[1] // 2 for right in rights]
            near += rights
            plan.append((len(outs), sizes, total))
            total += sum(sizes)
        outs.append(shape_of((groups[0][0].shape[1], total), LOW))
    extra = [] if received is None else list(received)

    def kernel(half_ref, *refs):
        out_refs = refs[len(near) + len(extra) :]
        at = 0
        for bundle, sizes, offset in plan:
            left = refs[at][...]
            for i, size in enumerate(sizes):
                here = slice(offset, offset + size)
                start = pl.multiple_of(half_ref[0] * size, 128)
                res = dot_tn(left, refs[at + 1 + i][:, pl.ds(start, size)])
                if extra:
                    res = res + refs[len(near) + bundle][:, here].astype(F32)
                out_refs[bundle][:, here] = res.astype(LOW)
                offset += size
            at += 1 + len(sizes)

    return call(kernel, half, near + extra, [], outs, [], 3 * len(plan), 16)


def tie(value, *others):
    others = [other for other in others if other is not None]
    return lax.optimization_barrier((value, *others))[0] if others else value


def place_of():
    f = lax.axis_index("fsdp")
    r = lax.axis_index("rep")
    return (f // 2, f % 2, r // 2, r % 2)


def z_flip(bit):
    return lambda z, y, x, c: (z ^ bit, y, x, c)


def pick(array, index, axis):
    return lax.dynamic_index_in_dim(array, index, axis, keepdims=False)


def add_low(one, two):
    return (one.astype(F32) + two.astype(F32)).astype(LOW)


def join_halves(left, right, widths):
    out, offset = [], 0
    for width in widths:
        here = slice(offset, offset + width // 2)
        out.append(jnp.concatenate([left[:, here], right[:, here]], axis=1))
        offset += width // 2
    return out


def own_piece(link, shards):
    _, _, x, c = link.place
    rows = shards[0].shape[0] // 2
    return jnp.concatenate(
        [
            lax.dynamic_slice(
                shard, (x * rows, c * (shard.shape[1] // 2)), (rows, shard.shape[1] // 2)
            )
            for shard in shards
        ],
        axis=1,
    )


class Gather:
    def __init__(self, link, shards, *after, extra=None):
        self.link = link
        grid = self.grid = link.grid
        own = own_piece(link, shards)
        rows = own.shape[0]
        if extra is not None:
            extra = jnp.pad(extra, ((0, rows - extra.shape[0]), (0, 128 - extra.shape[1])))
            own = jnp.concatenate([own, extra], axis=1)
        own = tie(own, *after)
        self.pair = jnp.stack([own, send(grid, own, z_flip(1))])
        self.base = None

    def long(self, *after):
        pair = tie(self.pair, *after)
        self.base = jnp.concatenate([self.pair, send(self.grid, pair, z_flip(2))])
        return self.base

    def near(self, *after):
        base = tie(self.base, *after)
        self.one = send(self.grid, base, first_flip)
        self.two = send(self.grid, base, second_flip)
        return self.one

    def far(self, *after):
        self.three = send(self.grid, tie(self.one, *after), second_flip)
        return self.three

    def extras(self, shape):
        rows, cols = shape
        z, y, x, c = self.link.place
        zs = self.grid.zs
        keep = [part[:, :rows, -128:][:, :, :cols] for part in (self.base, self.one, self.two, self.three)]
        near = keep[0]
        far = jnp.where(c == 0, keep[2], keep[1])
        blocks = []
        for zz in range(zs):
            k = jnp.bitwise_xor(z, zz)
            for yy in range(2):
                blocks.append(jnp.where(y == yy, pick(near, k, 0), pick(far, k, 0)))
        return jnp.concatenate(blocks, axis=1)

    def whole(self, *after):
        near = [self.base, self.one, self.two, self.three]
        return near + [send(self.grid, part, core_flip) for part in near]


class Offloaded:
    def __init__(self, link, shards):
        self.own = own_piece(link, shards)

    def whole(self, *after):
        return [lax.all_gather(tie(self.own, *after), AXES, axis=0)]


class PlainGather:
    pair = base = one = three = None

    def long(self, *after):
        return None

    def __init__(self, link, shards, *after, extra=None):
        self.shards, self.extra = shards, extra

    def extras(self, shape):
        return lax.all_gather(self.extra, "fsdp", axis=1, tiled=True)

    def near(self, *after):
        return None

    def far(self, *after):
        return None

    def whole(self, *after):
        full = [lax.all_gather(shard, "fsdp", axis=0, tiled=True) for shard in self.shards]
        halves = [
            jnp.concatenate([jnp.split(weight, 2, axis=1)[c] for weight in full], axis=1)
            for c in range(2)
        ]
        return [jnp.stack(halves)]


class Reduce:
    def __init__(self, link, half, widths):
        self.link, self.widths = link, widths
        z, y, x, c = link.place
        zs = self.link.grid.zs
        rows, cols = half.shape[0] // (4 * zs), half.shape[1]
        view = half.reshape(zs, 2, 2, rows, cols)
        self.keep = jnp.where(c == 0, pick(view, y, 1), pick(view, x, 2))
        away = jnp.where(c == 0, pick(view, 1 - y, 1), pick(view, 1 - x, 2))
        self.got = send(self.link.grid, away, second_flip)

    def one(self, *after):
        z, y, x, c = self.link.place
        part = add_low(self.keep, tie(self.got, *after))
        b = jnp.where(c == 0, x, y)
        self.keep = pick(part, b, 1)
        away = pick(part, 1 - b, 1)
        self.got = send(self.link.grid, away, first_flip)
        return away

    def two(self, *after):
        z = self.link.place[0]
        part = add_low(self.keep, tie(self.got, *after))
        self.keep = lax.dynamic_slice_in_dim(part, z // 2 * 2, 2, 0)
        away = lax.dynamic_slice_in_dim(part, (1 - z // 2) * 2, 2, 0)
        self.got = send(self.link.grid, away, z_flip(2))
        return away

    def next(self, *after):
        z = self.link.place[0]
        part = add_low(self.keep, tie(self.got, *after))
        self.keep = pick(part, z % 2, 0)
        away = pick(part, 1 - z % 2, 0)
        self.got = send(self.link.grid, away, z_flip(1))
        return away

    def three(self, *after):
        self.keep = add_low(self.keep, tie(self.got, *after))
        self.got = send(self.link.grid, self.keep, x_flip)
        return self.keep

    def four(self, *after):
        x = self.link.place[2]
        self.got = tie(self.got, *after)
        self.keep = jnp.concatenate(
            [jnp.where(x == 0, self.keep, self.got), jnp.where(x == 0, self.got, self.keep)],
            axis=0,
        )
        self.got = send(self.link.grid, self.keep, core_flip)
        return self.keep

    def out(self, *after):
        c = self.link.place[3]
        self.got = tie(self.got, *after)
        left = jnp.where(c == 0, self.keep, self.got).astype(F32)
        right = jnp.where(c == 0, self.got, self.keep).astype(F32)
        return join_halves(left, right, self.widths)


class PlainReduce:
    def __init__(self, link, half, widths):
        self.half, self.widths = half, widths

    def one(self, *after):
        return None

    two = next = three = four = one

    def out(self, *after):
        share = lax.psum_scatter(self.half, "fsdp", scatter_dimension=0, tiled=True)
        share = lax.psum(share, "rep").astype(F32)
        return join_halves(share[:, 0], share[:, 1], self.widths)


class Direct:
    gather, wide, reduce = Gather, Offloaded, Reduce

    def __init__(self, fsdp, rep):
        self.grid = Grid(fsdp, rep)
        self.place = place_of()
        self.at = jnp.stack(self.place).astype(jnp.int32)
        self.mine = self.at[3:4]
        self.other = 1 - self.mine

    def others(self, bundles, *after):
        away = weight_grads(tie(self.other, *after), bundles, None)
        return away, [send(self.grid, half, core_flip) for half in away]

    def mine_of(self, bundles, got, *after):
        return weight_grads(tie(self.mine, *after), bundles, got)

    def reduce_gains(self, value, *after):
        z, y = self.place[:2]
        flips = (core_flip, x_flip, y_flip, z_flip(1), z_flip(2))
        for flip, late in zip(flips, after):
            value = value + tie(send(self.grid, value, flip), late)
        share = value.shape[1] // (2 * self.grid.zs)
        return lax.dynamic_slice_in_dim(value, (z * 2 + y) * share, share, 1)


class Plain:
    gather, wide, reduce = PlainGather, PlainGather, PlainReduce

    def __init__(self):
        self.at = jnp.zeros((4,), jnp.int32)

    def others(self, bundles, *after):
        return [None], None

    def mine_of(self, bundles, got, *after):
        halves = [weight_grads(jnp.full((1,), c, jnp.int32), bundles, None) for c in range(2)]
        return [jnp.stack(pair, axis=1) for pair in zip(*halves)]

    def reduce_gains(self, value, *after):
        share = lax.psum_scatter(value, "fsdp", scatter_dimension=1, tiled=True)
        return lax.psum(share, "rep")


def rope_tables(positions):
    even_steps = jnp.arange(0, HEAD_DIM, 2).astype(F32)
    inverse = jnp.exp(even_steps * (-math.log(10000.0) / HEAD_DIM))
    angles = positions.astype(F32)[:, None] * inverse
    cosine, sine = jnp.cos(angles), jnp.sin(angles)
    return jnp.concatenate([cosine] * 4, axis=1), jnp.concatenate([-sine, sine] * 2, axis=1)


def body(
    fsdp,
    rep,
    tokens,
    cotangent,
    seq_lengths,
    token_positions,
    first_query,
    first_key,
    first_value,
    first_output,
    first_gate,
    first_up,
    first_down,
    first_attngain,
    first_ffngain,
    second_query,
    second_key,
    second_value,
    second_output,
    second_gate,
    second_up,
    second_down,
    second_attngain,
    second_ffngain,
):
    _, rows, width = tokens.shape
    wide = first_gate.shape[1]
    low_tokens = tokens.reshape(rows, width)
    low_cot = cotangent.reshape(rows, width)
    link = Direct(fsdp, rep) if (fsdp, rep) == (8, 4) else Plain()
    at = jnp.concatenate([link.at, seq_lengths.astype(jnp.int32)])
    cosine, sine = rope_tables(token_positions.reshape(rows))
    pairs = width // PAIR
    split = pairs // 2
    attn_widths, open_widths = (width,) * 3, (width, wide, wide)

    own_gains = jnp.stack([first_attngain, first_ffngain, second_attngain, second_ffngain])
    heads_one = link.gather(link, (first_query, first_key, first_value), extra=own_gains)
    heads_one.long()
    open_one = link.gather(link, (first_output, first_gate, first_up), heads_one.base)
    heads_one.near()
    open_one.long(heads_one.one)
    far = heads_one.far()
    heads_two = link.wide(link, (second_query, second_key, second_value)).whole(far)
    open_one.near(far)
    down_one = link.gather(link, (first_down,), heads_one.base)
    parts = heads_one.whole()
    q1, k1, v1 = project_heads(at, low_tokens, parts, cosine, sine)
    gains = heads_one.extras(own_gains.shape).astype(F32)
    heads_one = parts
    attn_one, ffn_one, attn_two, ffn_two = (gains[i : i + 1] for i in range(4))
    down_one.long(q1)
    half = attend(at, q1, k1, v1, 0, split)
    open_one.far(half[0])
    down_one.near(half[0])
    open_two = link.gather(link, (second_output, second_gate, second_up), half[0])
    o1, log1 = attend(
        at, tie(q1, open_one.one, down_one.base), k1, v1, split, pairs - split, half
    )
    open_one = open_one.whole()
    open_two.long(o1)
    r1, h1, gate1, up1, z1 = open_block(at, o1, low_tokens, attn_one, open_one, wide)
    down_one.far(r1)
    open_two.near(r1)
    down_two = link.gather(link, (second_down,), r1)
    down_one = down_one.whole()
    r2, first_out, n1 = close_first(at, z1, r1, gains, down_one)
    down_two.long(first_out)
    q2, k2, v2 = project_heads(at, n1, heads_two, cosine, sine)
    open_two.far(q2)
    down_two.near(q2)
    half = attend(at, q2, k2, v2, 0, split)
    down_two.far(half[0])
    o2, log2 = attend(at, tie(q2, open_two.three, down_two.one), k2, v2, split, pairs - split, half)
    open_two = open_two.whole()
    r3, h2, gate2, up2, z2 = open_block(at, o2, first_out, ffn_two, open_two, wide)
    down_two = down_two.whole()

    dgate2, dup2, dr3, dr3_low, do2, gain_d = feed_back(
        at, low_cot, low_cot, gate2, up2, r3, ffn_two, open_two, down_two, False
    )
    bundles = [[(o2, [dr3_low]), (h2, [dgate2, dup2])], [(z2, [low_cot])]]
    away, got = link.others(bundles, dr3)
    half = attend_back(at, tie(q2, away[0]), k2, v2, o2, log2, do2, cosine, sine, 0, split)
    sent = link.mine_of(bundles, got, half[0])
    open_g2, down_g2 = (
        link.reduce(link, grad, widths) for grad, widths in zip(sent, (open_widths, (width,)))
    )
    dq2, dk2, dv2 = attend_back(
        at, tie(q2, sent[0]), k2, v2, o2, log2, do2, cosine, sine, split, pairs - split, half
    )
    bundles = [[(n1, [dq2, dk2, dv2])]]
    part = down_g2.one(dq2)
    away, got = link.others(bundles, part)
    dr2, dr2_low, gain_c, gain_b = heads_back_second(
        tie(at, away[0]),
        dq2,
        dk2,
        dv2,
        dr3,
        first_out,
        r2,
        jnp.concatenate([attn_two, ffn_one]),
        heads_two,
    )
    part = (open_g2.one(dr2), down_g2.two(dr2))
    sent = link.mine_of(bundles, got, dr2, *part)
    heads_g2 = link.reduce(link, sent[0], attn_widths)

    dgate1, dup1, dr1, dr1_low, do1, gain_a = feed_back(
        tie(at, sent[0]), dr2, dr2_low, gate1, up1, r1, attn_one, open_one, down_one, True
    )
    part = (open_g2.two(dr1), heads_g2.one(dr1), down_g2.next(dr1))
    bundles = [[(o1, [dr1_low]), (h1, [dgate1, dup1])], [(z1, [dr2_low])]]
    away, got = link.others(bundles, dr1, *part)
    second_out = close_second(tie(at, away[0]), z2, r3, down_two)
    part = (heads_g2.two(second_out), open_g2.next(second_out), down_g2.three(second_out))
    sent = link.mine_of(bundles, got, second_out, *part)
    open_g1, down_g1 = (
        link.reduce(link, grad, widths) for grad, widths in zip(sent, (open_widths, (width,)))
    )
    gain_grads = jnp.stack([jnp.sum(share, axis=0) for share in (gain_a, gain_b, gain_c, gain_d)])
    half = attend_back(at, tie(q1, sent[0]), k1, v1, o1, log1, do1, cosine, sine, 0, split)
    part = (down_g1.one(half[0]), heads_g2.next(half[0]), open_g2.three(half[0]), down_g2.four(half[0]))
    dq1, dk1, dv1 = attend_back(
        at, tie(q1, *part), k1, v1, o1, log1, do1, cosine, sine, split, pairs - split, half
    )
    part = (open_g1.one(dq1), down_g1.two(dq1), heads_g2.three(dq1), open_g2.four(dq1))
    bundles = [[(low_tokens, [dq1, dk1, dv1])]]
    away, got = link.others(bundles, *part)
    heads_g2.four(away[0])
    part = (down_g1.next(away[0]), open_g1.two(away[0]))
    (down_g2,) = down_g2.out(away[0])
    output_g2, gate_g2, up_g2 = open_g2.out(away[0])
    sent = link.mine_of(bundles, got, *part, down_g2, output_g2, gate_g2, up_g2)
    heads_g1 = link.reduce(link, sent[0], attn_widths)
    input_grad = heads_back_first(tie(at, sent[0]), dq1, dk1, dv1, dr1, heads_one)
    part = (heads_g1.one(input_grad), open_g1.next(input_grad), down_g1.three(input_grad))
    query_g2, key_g2, value_g2 = heads_g2.out(*part)
    part = (heads_g1.two(query_g2), open_g1.three(query_g2), down_g1.four(query_g2))
    heads_g1.next(part[0])
    open_g1.four(part[0])
    (down_g1,) = down_g1.out(part[0])
    part = heads_g1.three()
    output_g1, gate_g1, up_g1 = open_g1.out(part)
    gain_grads = link.reduce_gains(gain_grads, second_out, half[0], dq1, sent[0], input_grad)
    heads_g1.four()
    query_g1, key_g1, value_g1 = heads_g1.out()
    return (
        first_out.reshape(tokens.shape),
        second_out.reshape(tokens.shape),
        input_grad.reshape(tokens.shape),
        query_g1,
        key_g1,
        value_g1,
        output_g1,
        gate_g1,
        up_g1,
        down_g1,
        gain_grads[0],
        gain_grads[1],
        query_g2,
        key_g2,
        value_g2,
        output_g2,
        gate_g2,
        up_g2,
        down_g2,
        gain_grads[2],
        gain_grads[3],
    )


def solution(mesh):
    per_seq = P(("fsdp", "rep"))
    shard = P("fsdp")
    return jax.shard_map(
        functools.partial(body, mesh.shape["fsdp"], mesh.shape["rep"]),
        mesh=mesh,
        in_specs=(per_seq,) * 4 + (shard,) * 18,
        out_specs=(per_seq,) * 3 + (shard,) * 18,
        check_vma=False,
    )
```

```python
import functools
import math

import jax
import jax.numpy as jnp
from jax import lax
from jax.experimental import pallas as pl
from jax.experimental.pallas import tpu as pltpu
from jax.sharding import PartitionSpec as P

HEAD_DIM = 64

epsilon = 1e-06
masked_score = -1e30


class Grid:
    def __init__(self, fsdp, rep):
        self.zs = fsdp // 2
        self.rep = rep

    def flat(self, z, y, x, c):
        return (z * 2 + y) * self.rep + x * 2 + c

    def pairs(self, move):
        out = []
        for z in range(self.zs):
            for y in range(2):
                for x in range(2):
                    for c in range(2):
                        out.append((self.flat(z, y, x, c), self.flat(*move(z, y, x, c))))
        return out


AXES = ("fsdp", "rep")


def send(grid, value, move):
    return lax.ppermute(value, AXES, grid.pairs(move))


def first_flip(z, y, x, c):
    return (z, y, 1 - x, c) if c == 0 else (z, 1 - y, x, c)


def second_flip(z, y, x, c):
    return (z, 1 - y, x, c) if c == 0 else (z, y, 1 - x, c)


def core_flip(z, y, x, c):
    return (z, y, x, 1 - c)


def x_flip(z, y, x, c):
    return (z, y, 1 - x, c)


def y_flip(z, y, x, c):
    return (z, 1 - y, x, c)

BLOCK = 256
PAIR = 2 * HEAD_DIM
VMEM = 32 * 1024 * 1024
F32 = jnp.float32
LOW = jnp.bfloat16


def dot(one, two):
    return jnp.dot(one, two, preferred_element_type=F32)


def dot_nt(one, two):
    return lax.dot_general(one, two, (((1,), (1,)), ((), ())), preferred_element_type=F32)


def dot_tn(one, two):
    return lax.dot_general(one, two, (((0,), (0,)), ((), ())), preferred_element_type=F32)


def inverse_rms(values):
    return lax.rsqrt(jnp.mean(values * values, axis=-1, keepdims=True) + epsilon)


def norm_back(values, scales, upstream):
    inv = inverse_rms(values)
    weighted = upstream * scales
    inner = jnp.mean(weighted * values, axis=-1, keepdims=True)
    return inv * weighted - values * (inv * inv * inv) * inner, upstream * values * inv


def fold_rows(values):
    return jnp.sum(values.reshape(values.shape[0] // 8, 8, values.shape[1]), axis=0)


def silu_parts(gate):
    sig = 0.5 * jnp.tanh(0.5 * gate) + 0.5
    return sig, gate * sig


def piece_place(at_ref, which, k):
    z, y, x, c = at_ref[0], at_ref[1], at_ref[2], at_ref[3]
    cc = c if which < 4 else 1 - c
    first, second = which % 2, (which % 4) // 2
    flip_x = jnp.where(cc == 0, first, second)
    flip_y = jnp.where(cc == 0, second, first)
    return jnp.bitwise_xor(z, k) * 2 + jnp.where(flip_y == 1, 1 - y, y), jnp.where(flip_x == 1, 1 - x, x), cc


def slabs(at_ref, pieces):
    count, rows, _ = pieces[0].shape
    if len(pieces) == 1:
        return [(pieces[0].at[i], i // 2 * rows, i % 2) for i in range(count)], rows
    out = []
    for which in range(8):
        for k in range(count):
            shard, x, c = piece_place(at_ref, which, k)
            row = pl.multiple_of(shard * (2 * rows) + x * rows, 16)
            out.append((pieces[which].at[k], row, c))
    return out, rows


def weight_copies(at_ref, pieces, w_refs, sems):
    copies = []
    places, rows = slabs(at_ref, pieces)
    for slab, row, c in places:
        offset = 0
        for w_ref in w_refs:
            half = w_ref.shape[1] // 2
            col = c * half if isinstance(c, int) else pl.multiple_of(c * half, 128)
            copies.append(
                pltpu.make_async_copy(
                    slab.at[:, pl.ds(offset, half)],
                    w_ref.at[pl.ds(row, rows), pl.ds(col, half)],
                    sems.at[len(copies)],
                )
            )
            offset += half
    return copies


def weight_scratch(pieces, widths):
    count, rows, _ = pieces[0].shape
    tall = count * rows // 2 if len(pieces) == 1 else count * 4 * rows
    copies = len(pieces) * count * len(widths)
    return [pltpu.VMEM((tall, width), LOW) for width in widths] + [
        pltpu.SemaphoreType.DMA((copies,))
    ]


def start_all(copies):
    for copy in copies:
        copy.start()
    return copies


def wait_all(copies):
    for copy in copies:
        copy.wait()


ANYWHERE = pl.BlockSpec(memory_space=pl.ANY)
HELD = pl.BlockSpec(memory_space=pltpu.HBM)
NEAR = pl.BlockSpec(memory_space=pltpu.VMEM)
SCALARS = pl.BlockSpec(memory_space=pltpu.SMEM)
MIB = 1024 * 1024


def cost(micros):
    return pl.CostEstimate(
        flops=int(micros * 1.1e9), bytes_accessed=int(micros * 1e5), transcendentals=0
    )


def call(kernel, at, near, weights, outs, scratch, micros, room):
    weights = [pltpu.with_memory_space_constraint(weight, pltpu.HBM) for weight in weights]
    return pl.pallas_call(
        kernel,
        out_shape=outs,
        in_specs=[SCALARS] + [NEAR] * len(near) + [HELD] * len(weights),
        out_specs=jax.tree.map(lambda _: NEAR, outs),
        scratch_shapes=scratch,
        compiler_params=pltpu.CompilerParams(vmem_limit_bytes=room * MIB),
        cost_estimate=cost(micros),
    )(at, *near, *weights)


def shape_of(shape, dtype):
    return jax.ShapeDtypeStruct(shape, dtype)


def blocks(rows):
    return [slice(first, first + BLOCK) for first in range(0, rows, BLOCK)]


def pair_spec(rows, first_pair):
    return pl.BlockSpec((rows, PAIR), lambda p, at: (0, p + first_pair))


def logs_spec(rows, first_pair):
    return pl.BlockSpec((1, 16, rows), lambda p, at: (p + first_pair, 0, 0))


def whole_spec(shape):
    return pl.BlockSpec(shape, lambda i, at: (0,) * len(shape))


def call_pairs(kernel, at, arrays, specs, outs, out_specs, scratch, steps, micros, aliases):
    arrays = [pltpu.with_memory_space_constraint(array, pltpu.HBM) for array in arrays]
    outs = [pltpu.HBM(out.shape, out.dtype) for out in outs]
    return pl.pallas_call(
        kernel,
        out_shape=outs,
        grid_spec=pltpu.PrefetchScalarGridSpec(
            num_scalar_prefetch=1,
            grid=(steps,),
            in_specs=specs,
            out_specs=out_specs,
            scratch_shapes=scratch,
        ),
        input_output_aliases=aliases,
        compiler_params=pltpu.CompilerParams(vmem_limit_bytes=16 * MIB),
        cost_estimate=cost(micros),
    )(at, *arrays)


def turn_lanes(values, lane):
    return jnp.where(
        (lane & (HEAD_DIM - 1)) < HEAD_DIM // 2,
        pltpu.roll(values, PAIR - HEAD_DIM // 2, 1),
        pltpu.roll(values, HEAD_DIM // 2, 1),
    )


def project_heads(at, inputs, pieces, cosine, sine):
    rows, width = inputs.shape
    n = len(pieces)

    def kernel(at_ref, a_ref, cos_ref, sin_ref, *refs):
        parts, (q_ref, k_ref, v_ref), (*w_refs, sems) = refs[:n], refs[n : n + 3], refs[n + 3 :]
        wait_all(start_all(weight_copies(at_ref, parts, w_refs, sems)))
        lane = lax.broadcasted_iota(jnp.int32, (BLOCK, PAIR), 1)
        for block in blocks(rows):
            a = a_ref[block, :]
            cos, sin = cos_ref[block, :], sin_ref[block, :]
            for first in range(0, width, 2 * PAIR):
                q = dot(a, w_refs[0][:, first : first + 2 * PAIR])
                k = dot(a, w_refs[1][:, first : first + 2 * PAIR])
                v = dot(a, w_refs[2][:, first : first + 2 * PAIR])
                for t in range(2):
                    here = slice(first + t * PAIR, first + (t + 1) * PAIR)
                    q_pair = q[:, t * PAIR : (t + 1) * PAIR]
                    k_pair = k[:, t * PAIR : (t + 1) * PAIR]
                    q_pair = q_pair * cos + turn_lanes(q_pair, lane) * sin
                    q_ref[block, here] = (q_pair * HEAD_DIM**-0.5).astype(LOW)
                    k_ref[block, here] = (k_pair * cos + turn_lanes(k_pair, lane) * sin).astype(LOW)
                v_ref[block, first : first + 2 * PAIR] = v.astype(LOW)

    return call(
        kernel,
        at,
        [inputs, cosine, sine],
        pieces,
        [shape_of((rows, width), LOW)] * 3,
        weight_scratch(pieces, (width,) * 3),
        8,
        16,
    )


def head_masks(head, lane):
    own = lane < HEAD_DIM if head == 0 else lane >= HEAD_DIM
    return own, lane == (HEAD_DIM if head == 0 else 0)


def attend(at, queries, key_rows, value_rows, first_pair, pairs, before=()):
    rows, width = queries.shape
    every = width // PAIR

    def kernel(at_ref, q_ref, k_ref, v_ref, *refs):
        o_ref, lse_ref = refs[len(before) :]
        lane = lax.broadcasted_iota(jnp.int32, (rows, PAIR), 1)
        row = lax.broadcasted_iota(jnp.int32, (rows, PAIR), 0)
        bias = jnp.where(row < at_ref[4], 0.0, masked_score)
        q, k, v = q_ref[...].astype(F32), k_ref[...].astype(F32), v_ref[...].astype(F32)
        below = lax.broadcasted_iota(jnp.int32, (BLOCK, BLOCK), 0) >= lax.broadcasted_iota(
            jnp.int32, (BLOCK, BLOCK), 1
        )
        heads = []
        for head in range(2):
            own, mark = head_masks(head, lane)
            heads.append(
                (
                    jnp.where(own, q, jnp.where(mark, 1.0, 0.0)).astype(LOW),
                    jnp.where(own, k, jnp.where(mark, bias, 0.0)).astype(LOW),
                    jnp.where(own, v, 1.0).astype(LOW),
                )
            )
        lane_here = lane[:BLOCK]
        for first in range(0, rows, BLOCK):
            end = first + BLOCK
            mixed, logs = [], []
            for qh, kh, vh in heads:
                scores = [
                    dot_nt(qh[first:end], kh[start : start + BLOCK]) for start in range(0, end, BLOCK)
                ]
                scores[-1] = jnp.where(below, scores[-1], masked_score)
                top = functools.reduce(jnp.maximum, scores)
                top = jnp.max(top, axis=-1, keepdims=True)
                weights = [jnp.exp(part - top).astype(LOW) for part in scores]
                weights = jnp.concatenate(weights, axis=1) if first else weights[0]
                both = dot(weights, vh[:end])
                total = pltpu.roll(both, HEAD_DIM, 1)
                mixed.append(both / total)
                logs.append(top + jnp.log(total))
            o_ref[first:end, :] = jnp.where(lane_here < HEAD_DIM, mixed[0], mixed[1]).astype(LOW)
            turned = jnp.where(lane_here < HEAD_DIM, logs[0], logs[1]).T
            lse_ref[0, 0:8, first:end] = turned[0:8]
            lse_ref[0, 8:16, first:end] = turned[HEAD_DIM : HEAD_DIM + 8]

    return call_pairs(
        kernel,
        at,
        [queries, key_rows, value_rows, *before],
        [pair_spec(rows, first_pair)] * 3 + [ANYWHERE] * len(before),
        [shape_of((rows, width), LOW), shape_of((every, 16, rows), F32)],
        [pair_spec(rows, first_pair), logs_spec(rows, first_pair)],
        [],
        pairs,
        4 * pairs,
        {4 + i: i for i in range(len(before))},
    )


def attend_back(
    at, queries, key_rows, value_rows, mixed, logs, upstream, cosine, sine, first_pair, pairs, before=()
):
    rows, width = queries.shape

    def kernel(at_ref, q_ref, k_ref, v_ref, o_ref, lse_ref, g_ref, cos_ref, sin_ref, *refs):
        dq_ref, dk_ref, dv_ref, sum_ref = refs[len(before) :]
        lane = lax.broadcasted_iota(jnp.int32, (rows, PAIR), 1)
        row = lax.broadcasted_iota(jnp.int32, (rows, PAIR), 0)
        bias = jnp.where(row < at_ref[4], 0.0, masked_score)
        q, k, v = q_ref[...].astype(F32), k_ref[...].astype(F32), v_ref[...].astype(F32)
        q_low, k_low, g_low = q_ref[...], k_ref[...], g_ref[...]
        above = lax.broadcasted_iota(jnp.int32, (BLOCK, BLOCK), 0) <= lax.broadcasted_iota(
            jnp.int32, (BLOCK, BLOCK), 1
        )
        turned = (g_low.astype(F32) * o_ref[...].astype(F32)).T
        cos, sin = cos_ref[...], sin_ref[...]

        def unrotate(values, first, end):
            moved = values * sin[first:end]
            return values * cos[first:end] + turn_lanes(moved, lane[first:end])

        key_parts, value_parts = [], []
        for head in range(2):
            own, mark = head_masks(head, lane)
            qh = jnp.where(own, q, jnp.where(mark, 1.0, 0.0)).astype(LOW)
            kh = jnp.where(own, k, jnp.where(mark, bias, 0.0)).astype(LOW)
            vh = jnp.where(own, v, 0.0).astype(LOW)
            delta = jnp.sum(
                turned[head * HEAD_DIM : (head + 1) * HEAD_DIM], axis=0, keepdims=True
            )
            lse = lse_ref[0, head * 8 : head * 8 + 1, :]
            key_parts.append([])
            value_parts.append([])
            for first in range(0, rows, BLOCK):
                end = first + BLOCK
                scores = dot_nt(kh[first:end], qh[first:])
                soft = jnp.exp(scores - lse[:, first:])
                edge = jnp.where(above, soft[:, :BLOCK], 0.0)
                if end < rows:
                    soft = jnp.concatenate([edge, soft[:, BLOCK:]], axis=1)
                else:
                    soft = edge
                grad = dot_nt(vh[first:end], g_low[first:])
                grad = (soft * (grad - delta[:, first:])).astype(LOW)
                value_parts[head].append(dot(soft.astype(LOW), g_low[first:]))
                key_parts[head].append(dot(grad, q_low[first:]))
                added = dot_tn(grad, k_low[first:end])
                if first == 0:
                    sum_ref[head] = added
                else:
                    sum_ref[head, first:, :] += added
        lane_here = lane[:BLOCK]
        for step in range(rows // BLOCK):
            first, end = step * BLOCK, (step + 1) * BLOCK
            dk = jnp.where(lane_here < HEAD_DIM, key_parts[0][step], key_parts[1][step])
            dv = jnp.where(lane_here < HEAD_DIM, value_parts[0][step], value_parts[1][step])
            dq = jnp.where(lane_here < HEAD_DIM, sum_ref[0, first:end, :], sum_ref[1, first:end, :])
            dk_ref[first:end, :] = unrotate(dk, first, end).astype(LOW)
            dq_ref[first:end, :] = unrotate(dq * HEAD_DIM**-0.5, first, end).astype(LOW)
            dv_ref[first:end, :] = dv.astype(LOW)

    return call_pairs(
        kernel,
        at,
        [queries, key_rows, value_rows, mixed, logs, upstream, cosine, sine, *before],
        [pair_spec(rows, first_pair)] * 4
        + [logs_spec(rows, first_pair), pair_spec(rows, first_pair)]
        + [whole_spec((rows, PAIR))] * 2
        + [ANYWHERE] * len(before),
        [shape_of((rows, width), LOW)] * 3,
        [pair_spec(rows, first_pair)] * 3,
        [pltpu.VMEM((2, rows, PAIR), F32)],
        pairs,
        5 * pairs,
        {9 + i: i for i in range(len(before))},
    )


def open_block(at, mixed, resid, gain, pieces, wide):
    rows, width = mixed.shape
    n = len(pieces)

    def kernel(at_ref, o_ref, resid_ref, gain_ref, *refs):
        parts, outs, (*w_refs, sems) = refs[:n], refs[n : n + 5], refs[n + 5 :]
        r_ref, hl_ref, gate_ref, up_ref, z_ref = outs
        wait_all(start_all(weight_copies(at_ref, parts, w_refs, sems)))
        for block in blocks(rows):
            r = resid_ref[block, :].astype(F32) + dot(o_ref[block, :], w_refs[0][...])
            r_ref[block, :] = r
            hl = (r * inverse_rms(r) * gain_ref[...]).astype(LOW)
            hl_ref[block, :] = hl
            for first in range(0, wide, BLOCK):
                here = slice(first, first + BLOCK)
                gate = dot(hl, w_refs[1][:, here])
                up = dot(hl, w_refs[2][:, here])
                gate_ref[block, here] = gate.astype(LOW)
                up_ref[block, here] = up.astype(LOW)
                z_ref[block, here] = (silu_parts(gate)[1] * up).astype(LOW)

    return call(
        kernel,
        at,
        [mixed, resid, gain],
        pieces,
        [shape_of((rows, width), F32), shape_of((rows, width), LOW)]
        + [shape_of((rows, wide), LOW)] * 3,
        weight_scratch(pieces, (width, wide, wide)),
        12,
        20,
    )


def close_first(at, hidden, resid, gains, pieces):
    rows, width = resid.shape
    n = len(pieces)

    def kernel(at_ref, z_ref, r_ref, gain_ref, *refs):
        parts, (r2_ref, out_ref, next_ref), (w_ref, sems) = refs[:n], refs[n : n + 3], refs[n + 3 :]
        wait_all(start_all(weight_copies(at_ref, parts, [w_ref], sems)))
        for block in blocks(rows):
            r = r_ref[block, :]
            r2 = r * inverse_rms(r) * gain_ref[0:1] + dot(z_ref[block, :], w_ref[...])
            r2_ref[block, :] = r2
            out = r2 * inverse_rms(r2) * gain_ref[1:2]
            out_ref[block, :] = out
            next_ref[block, :] = (out * inverse_rms(out) * gain_ref[2:3]).astype(LOW)

    return call(
        kernel,
        at,
        [hidden, resid, gains],
        pieces,
        [shape_of((rows, width), F32)] * 2 + [shape_of((rows, width), LOW)],
        weight_scratch(pieces, (width,)),
        8,
        16,
    )


def close_second(at, hidden, resid, pieces):
    rows, width = resid.shape
    n = len(pieces)

    def kernel(at_ref, z_ref, r_ref, *refs):
        parts, out_ref, (w_ref, sems) = refs[:n], refs[n], refs[n + 1 :]
        wait_all(start_all(weight_copies(at_ref, parts, [w_ref], sems)))
        for block in blocks(rows):
            out_ref[block, :] = r_ref[block, :] + dot(z_ref[block, :], w_ref[...])

    return call(
        kernel,
        at,
        [hidden, resid],
        pieces,
        shape_of((rows, width), F32),
        weight_scratch(pieces, (width,)),
        7,
        16,
    )


def feed_back(at, upstream, up_low, gate, up, resid, gain, pieces, down, post):
    rows, width = resid.shape
    wide = gate.shape[1]
    n, m = len(pieces), len(down)

    def kernel(at_ref, du_ref, dl_ref, gate_ref, up_ref, r_ref, gain_ref, *refs):
        parts, down_parts, refs = refs[:n], refs[n : n + m], refs[n + m :]
        dgate_ref, dup_ref, dr_ref, dlow_ref, do_ref, dgain_ref = refs[:6]
        *w_refs, sems, d_ref, d_sems = refs[6:]
        down_copies = start_all(weight_copies(at_ref, down_parts, [d_ref], d_sems))
        copies = start_all(weight_copies(at_ref, parts, w_refs, sems))
        wait_all(down_copies)
        for block in blocks(rows):
            dl = dl_ref[block, :]
            for first in range(0, wide, BLOCK):
                here = slice(first, first + BLOCK)
                dz = dot_nt(dl, d_ref[here, :])
                gate = gate_ref[block, here].astype(F32)
                sig, act = silu_parts(gate)
                dup_ref[block, here] = (dz * act).astype(LOW)
                dgate = dz * up_ref[block, here].astype(F32) * (sig + act * (1.0 - sig))
                dgate_ref[block, here] = dgate.astype(LOW)
        wait_all(copies)
        shares = None
        for block in blocks(rows):
            inward = dot_nt(dgate_ref[block, :], w_refs[1][...])
            inward = inward + dot_nt(dup_ref[block, :], w_refs[2][...])
            du = du_ref[block, :].astype(F32)
            if post:
                dr, share = norm_back(r_ref[block, :], gain_ref[...], du + inward)
            else:
                dr, share = norm_back(r_ref[block, :], gain_ref[...], inward)
                dr = du + dr
            dr_ref[block, :] = dr
            low = dr.astype(LOW)
            dlow_ref[block, :] = low
            do_ref[block, :] = dot_nt(low, w_refs[0][...]).astype(LOW)
            share = fold_rows(share)
            shares = share if shares is None else shares + share
        dgain_ref[...] = shares

    return call(
        kernel,
        at,
        [upstream, up_low, gate, up, resid, gain],
        [*pieces, *down],
        [shape_of((rows, wide), LOW)] * 2
        + [shape_of((rows, width), F32)]
        + [shape_of((rows, width), LOW)] * 2
        + [shape_of((8, width), F32)],
        weight_scratch(pieces, (width, wide, wide)) + weight_scratch(down, (width,)),
        24,
        18,
    )


def heads_inward(block, grad_refs, w_refs):
    inward = dot_nt(grad_refs[0][block, :], w_refs[0][...])
    inward = inward + dot_nt(grad_refs[1][block, :], w_refs[1][...])
    return inward + dot_nt(grad_refs[2][block, :], w_refs[2][...])


def heads_back_second(at, dq, dk, dv, upstream, first_out, resid_two, gains, pieces):
    rows, width = dq.shape
    n = len(pieces)

    def kernel(at_ref, dq_ref, dk_ref, dv_ref, du_ref, h_ref, r_ref, gain_ref, *refs):
        parts, refs = refs[:n], refs[n:]
        dr_ref, dlow_ref, ga_ref, gb_ref, *w_refs, sems = refs
        wait_all(start_all(weight_copies(at_ref, parts, w_refs, sems)))
        sums = [None, None]
        for block in blocks(rows):
            inward = heads_inward(block, (dq_ref, dk_ref, dv_ref), w_refs)
            back, share_a = norm_back(h_ref[block, :], gain_ref[0:1], inward)
            dr, share_b = norm_back(r_ref[block, :], gain_ref[1:2], du_ref[block, :] + back)
            dr_ref[block, :] = dr
            dlow_ref[block, :] = dr.astype(LOW)
            for i, share in enumerate((share_a, share_b)):
                share = fold_rows(share)
                sums[i] = share if sums[i] is None else sums[i] + share
        ga_ref[...] = sums[0]
        gb_ref[...] = sums[1]

    return call(
        kernel,
        at,
        [dq, dk, dv, upstream, first_out, resid_two, gains],
        pieces,
        [shape_of((rows, width), F32), shape_of((rows, width), LOW)]
        + [shape_of((8, width), F32)] * 2,
        weight_scratch(pieces, (width,) * 3),
        8,
        16,
    )


def heads_back_first(at, dq, dk, dv, upstream, pieces):
    rows, width = dq.shape
    n = len(pieces)

    def kernel(at_ref, dq_ref, dk_ref, dv_ref, du_ref, *refs):
        parts, (out_ref, *w_refs, sems) = refs[:n], refs[n:]
        wait_all(start_all(weight_copies(at_ref, parts, w_refs, sems)))
        for block in blocks(rows):
            out_ref[block, :] = du_ref[block, :] + heads_inward(
                block, (dq_ref, dk_ref, dv_ref), w_refs
            )

    return call(
        kernel,
        at,
        [dq, dk, dv, upstream],
        pieces,
        shape_of((rows, width), F32),
        weight_scratch(pieces, (width,) * 3),
        7,
        16,
    )


def weight_grads(half, bundles, received):
    near, plan, outs = [], [], []
    for groups in bundles:
        total = 0
        for left, rights in groups:
            near.append(left)
            sizes = [right.shape[1] // 2 for right in rights]
            near += rights
            plan.append((len(outs), sizes, total))
            total += sum(sizes)
        outs.append(shape_of((groups[0][0].shape[1], total), LOW))
    extra = [] if received is None else list(received)

    def kernel(half_ref, *refs):
        out_refs = refs[len(near) + len(extra) :]
        at = 0
        for bundle, sizes, offset in plan:
            left = refs[at][...]
            for i, size in enumerate(sizes):
                here = slice(offset, offset + size)
                start = pl.multiple_of(half_ref[0] * size, 128)
                res = dot_tn(left, refs[at + 1 + i][:, pl.ds(start, size)])
                if extra:
                    res = res + refs[len(near) + bundle][:, here].astype(F32)
                out_refs[bundle][:, here] = res.astype(LOW)
                offset += size
            at += 1 + len(sizes)

    return call(kernel, half, near + extra, [], outs, [], 3 * len(plan), 16)


def tie(value, *others):
    others = [other for other in others if other is not None]
    return lax.optimization_barrier((value, *others))[0] if others else value


def place_of():
    f = lax.axis_index("fsdp")
    r = lax.axis_index("rep")
    return (f // 2, f % 2, r // 2, r % 2)


def z_flip(bit):
    return lambda z, y, x, c: (z ^ bit, y, x, c)


def pick(array, index, axis):
    return lax.dynamic_index_in_dim(array, index, axis, keepdims=False)


def add_low(one, two):
    return (one.astype(F32) + two.astype(F32)).astype(LOW)


def join_halves(left, right, widths):
    out, offset = [], 0
    for width in widths:
        here = slice(offset, offset + width // 2)
        out.append(jnp.concatenate([left[:, here], right[:, here]], axis=1))
        offset += width // 2
    return out


def own_piece(link, shards):
    _, _, x, c = link.place
    rows = shards[0].shape[0] // 2
    return jnp.concatenate(
        [
            lax.dynamic_slice(
                shard, (x * rows, c * (shard.shape[1] // 2)), (rows, shard.shape[1] // 2)
            )
            for shard in shards
        ],
        axis=1,
    )


class Gather:
    def __init__(self, link, shards, *after, extra=None):
        self.link = link
        grid = self.grid = link.grid
        own = own_piece(link, shards)
        rows = own.shape[0]
        if extra is not None:
            extra = jnp.pad(extra, ((0, rows - extra.shape[0]), (0, 128 - extra.shape[1])))
            own = jnp.concatenate([own, extra], axis=1)
        own = tie(own, *after)
        self.pair = jnp.stack([own, send(grid, own, z_flip(1))])
        self.base = None

    def long(self, *after):
        pair = tie(self.pair, *after)
        self.base = jnp.concatenate([self.pair, send(self.grid, pair, z_flip(2))])
        return self.base

    def near(self, *after):
        base = tie(self.base, *after)
        self.one = send(self.grid, base, first_flip)
        self.two = send(self.grid, base, second_flip)
        return self.one

    def far(self, *after):
        self.three = send(self.grid, tie(self.one, *after), second_flip)
        return self.three

    def extras(self, shape):
        rows, cols = shape
        z, y, x, c = self.link.place
        zs = self.grid.zs
        keep = [part[:, :rows, -128:][:, :, :cols] for part in (self.base, self.one, self.two, self.three)]
        near = keep[0]
        far = jnp.where(c == 0, keep[2], keep[1])
        blocks = []
        for zz in range(zs):
            k = jnp.bitwise_xor(z, zz)
            for yy in range(2):
                blocks.append(jnp.where(y == yy, pick(near, k, 0), pick(far, k, 0)))
        return jnp.concatenate(blocks, axis=1)

    def whole(self, *after):
        near = [self.base, self.one, self.two, self.three]
        return near + [send(self.grid, part, core_flip) for part in near]


class Offloaded:
    def __init__(self, link, shards):
        self.own = own_piece(link, shards)

    def whole(self, *after):
        return [lax.all_gather(tie(self.own, *after), AXES, axis=0)]


class PlainGather:
    pair = base = one = three = None

    def long(self, *after):
        return None

    def __init__(self, link, shards, *after, extra=None):
        self.shards, self.extra = shards, extra

    def extras(self, shape):
        return lax.all_gather(self.extra, "fsdp", axis=1, tiled=True)

    def near(self, *after):
        return None

    def far(self, *after):
        return None

    def whole(self, *after):
        full = [lax.all_gather(shard, "fsdp", axis=0, tiled=True) for shard in self.shards]
        halves = [
            jnp.concatenate([jnp.split(weight, 2, axis=1)[c] for weight in full], axis=1)
            for c in range(2)
        ]
        return [jnp.stack(halves)]


class Reduce:
    def __init__(self, link, half, widths):
        self.link, self.widths = link, widths
        z, y, x, c = link.place
        zs = self.link.grid.zs
        rows, cols = half.shape[0] // (4 * zs), half.shape[1]
        view = half.reshape(zs, 2, 2, rows, cols)
        self.keep = jnp.where(c == 0, pick(view, y, 1), pick(view, x, 2))
        away = jnp.where(c == 0, pick(view, 1 - y, 1), pick(view, 1 - x, 2))
        self.got = send(self.link.grid, away, second_flip)

    def one(self, *after):
        z, y, x, c = self.link.place
        part = add_low(self.keep, tie(self.got, *after))
        b = jnp.where(c == 0, x, y)
        self.keep = pick(part, b, 1)
        away = pick(part, 1 - b, 1)
        self.got = send(self.link.grid, away, first_flip)
        return away

    def two(self, *after):
        z = self.link.place[0]
        part = add_low(self.keep, tie(self.got, *after))
        self.keep = lax.dynamic_slice_in_dim(part, z // 2 * 2, 2, 0)
        away = lax.dynamic_slice_in_dim(part, (1 - z // 2) * 2, 2, 0)
        self.got = send(self.link.grid, away, z_flip(2))
        return away

    def next(self, *after):
        z = self.link.place[0]
        part = add_low(self.keep, tie(self.got, *after))
        self.keep = pick(part, z % 2, 0)
        away = pick(part, 1 - z % 2, 0)
        self.got = send(self.link.grid, away, z_flip(1))
        return away

    def three(self, *after):
        self.keep = add_low(self.keep, tie(self.got, *after))
        self.got = send(self.link.grid, self.keep, x_flip)
        return self.keep

    def four(self, *after):
        x = self.link.place[2]
        self.got = tie(self.got, *after)
        self.keep = jnp.concatenate(
            [jnp.where(x == 0, self.keep, self.got), jnp.where(x == 0, self.got, self.keep)],
            axis=0,
        )
        self.got = send(self.link.grid, self.keep, core_flip)
        return self.keep

    def out(self, *after):
        c = self.link.place[3]
        self.got = tie(self.got, *after)
        left = jnp.where(c == 0, self.keep, self.got).astype(F32)
        right = jnp.where(c == 0, self.got, self.keep).astype(F32)
        return join_halves(left, right, self.widths)


class PlainReduce:
    def __init__(self, link, half, widths):
        self.half, self.widths = half, widths

    def one(self, *after):
        return None

    two = next = three = four = one

    def out(self, *after):
        share = lax.psum_scatter(self.half, "fsdp", scatter_dimension=0, tiled=True)
        share = lax.psum(share, "rep").astype(F32)
        return join_halves(share[:, 0], share[:, 1], self.widths)


class Direct:
    gather, wide, reduce = Gather, Offloaded, Reduce

    def __init__(self, fsdp, rep):
        self.grid = Grid(fsdp, rep)
        self.place = place_of()
        self.at = jnp.stack(self.place).astype(jnp.int32)
        self.mine = self.at[3:4]
        self.other = 1 - self.mine

    def others(self, bundles, *after):
        away = weight_grads(tie(self.other, *after), bundles, None)
        return away, [send(self.grid, half, core_flip) for half in away]

    def mine_of(self, bundles, got, *after):
        return weight_grads(tie(self.mine, *after), bundles, got)

    def reduce_gains(self, value, *after):
        z, y = self.place[:2]
        flips = (core_flip, x_flip, y_flip, z_flip(1), z_flip(2))
        for flip, late in zip(flips, after):
            value = value + tie(send(self.grid, value, flip), late)
        share = value.shape[1] // (2 * self.grid.zs)
        return lax.dynamic_slice_in_dim(value, (z * 2 + y) * share, share, 1)


class Plain:
    gather, wide, reduce = PlainGather, PlainGather, PlainReduce

    def __init__(self):
        self.at = jnp.zeros((4,), jnp.int32)

    def others(self, bundles, *after):
        return [None], None

    def mine_of(self, bundles, got, *after):
        halves = [weight_grads(jnp.full((1,), c, jnp.int32), bundles, None) for c in range(2)]
        return [jnp.stack(pair, axis=1) for pair in zip(*halves)]

    def reduce_gains(self, value, *after):
        share = lax.psum_scatter(value, "fsdp", scatter_dimension=1, tiled=True)
        return lax.psum(share, "rep")


def rope_tables(positions):
    even_steps = jnp.arange(0, HEAD_DIM, 2).astype(F32)
    inverse = jnp.exp(even_steps * (-math.log(10000.0) / HEAD_DIM))
    angles = positions.astype(F32)[:, None] * inverse
    cosine, sine = jnp.cos(angles), jnp.sin(angles)
    return jnp.concatenate([cosine] * 4, axis=1), jnp.concatenate([-sine, sine] * 2, axis=1)


def body(
    fsdp,
    rep,
    tokens,
    cotangent,
    seq_lengths,
    token_positions,
    first_query,
    first_key,
    first_value,
    first_output,
    first_gate,
    first_up,
    first_down,
    first_attngain,
    first_ffngain,
    second_query,
    second_key,
    second_value,
    second_output,
    second_gate,
    second_up,
    second_down,
    second_attngain,
    second_ffngain,
):
    _, rows, width = tokens.shape
    wide = first_gate.shape[1]
    low_tokens = tokens.reshape(rows, width)
    low_cot = cotangent.reshape(rows, width)
    link = Direct(fsdp, rep) if (fsdp, rep) == (8, 4) else Plain()
    at = jnp.concatenate([link.at, seq_lengths.astype(jnp.int32)])
    cosine, sine = rope_tables(token_positions.reshape(rows))
    pairs = width // PAIR
    split = pairs // 2
    attn_widths, open_widths = (width,) * 3, (width, wide, wide)

    own_gains = jnp.stack([first_attngain, first_ffngain, second_attngain, second_ffngain])
    heads_one = link.gather(link, (first_query, first_key, first_value), extra=own_gains)
    heads_one.long()
    open_one = link.gather(link, (first_output, first_gate, first_up), heads_one.base)
    heads_one.near()
    open_one.long(heads_one.one)
    far = heads_one.far()
    heads_two = link.wide(link, (second_query, second_key, second_value)).whole(far)
    open_one.near(far)
    down_one = link.gather(link, (first_down,), heads_one.base)
    parts = heads_one.whole()
    q1, k1, v1 = project_heads(at, low_tokens, parts, cosine, sine)
    gains = heads_one.extras(own_gains.shape).astype(F32)
    heads_one = parts
    attn_one, ffn_one, attn_two, ffn_two = (gains[i : i + 1] for i in range(4))
    down_one.long(q1)
    half = attend(at, q1, k1, v1, 0, split)
    open_one.far(half[0])
    down_one.near(half[0])
    open_two = link.gather(link, (second_output, second_gate, second_up), half[0])
    o1, log1 = attend(
        at, tie(q1, open_one.one, down_one.base), k1, v1, split, pairs - split, half
    )
    open_one = open_one.whole()
    open_two.long(o1)
    r1, h1, gate1, up1, z1 = open_block(at, o1, low_tokens, attn_one, open_one, wide)
    down_one.far(r1)
    open_two.near(r1)
    down_two = link.gather(link, (second_down,), r1)
    down_one = down_one.whole()
    r2, first_out, n1 = close_first(at, z1, r1, gains, down_one)
    down_two.long(first_out)
    q2, k2, v2 = project_heads(at, n1, heads_two, cosine, sine)
    open_two.far(q2)
    down_two.near(q2)
    half = attend(at, q2, k2, v2, 0, split)
    down_two.far(half[0])
    o2, log2 = attend(at, tie(q2, open_two.three, down_two.one), k2, v2, split, pairs - split, half)
    open_two = open_two.whole()
    r3, h2, gate2, up2, z2 = open_block(at, o2, first_out, ffn_two, open_two, wide)
    down_two = down_two.whole()

    dgate2, dup2, dr3, dr3_low, do2, gain_d = feed_back(
        at, low_cot, low_cot, gate2, up2, r3, ffn_two, open_two, down_two, False
    )
    bundles = [[(o2, [dr3_low]), (h2, [dgate2, dup2])], [(z2, [low_cot])]]
    away, got = link.others(bundles, dr3)
    half = attend_back(at, tie(q2, away[0]), k2, v2, o2, log2, do2, cosine, sine, 0, split)
    sent = link.mine_of(bundles, got, half[0])
    open_g2, down_g2 = (
        link.reduce(link, grad, widths) for grad, widths in zip(sent, (open_widths, (width,)))
    )
    dq2, dk2, dv2 = attend_back(
        at, tie(q2, sent[0]), k2, v2, o2, log2, do2, cosine, sine, split, pairs - split, half
    )
    bundles = [[(n1, [dq2, dk2, dv2])]]
    part = down_g2.one(dq2)
    away, got = link.others(bundles, part)
    dr2, dr2_low, gain_c, gain_b = heads_back_second(
        tie(at, away[0]),
        dq2,
        dk2,
        dv2,
        dr3,
        first_out,
        r2,
        jnp.concatenate([attn_two, ffn_one]),
        heads_two,
    )
    part = (open_g2.one(dr2), down_g2.two(dr2))
    sent = link.mine_of(bundles, got, dr2, *part)
    heads_g2 = link.reduce(link, sent[0], attn_widths)

    dgate1, dup1, dr1, dr1_low, do1, gain_a = feed_back(
        tie(at, sent[0]), dr2, dr2_low, gate1, up1, r1, attn_one, open_one, down_one, True
    )
    part = (open_g2.two(dr1), down_g2.next(dr1))
    bundles = [[(o1, [dr1_low]), (h1, [dgate1, dup1])], [(z1, [dr2_low])]]
    away, got = link.others(bundles, dr1, *part)
    second_out = close_second(tie(at, away[0]), z2, r3, down_two)
    part = (heads_g2.one(second_out), down_g2.three(second_out))
    sent = link.mine_of(bundles, got, second_out, *part)
    open_g1, down_g1 = (
        link.reduce(link, grad, widths) for grad, widths in zip(sent, (open_widths, (width,)))
    )
    gain_grads = jnp.stack([jnp.sum(share, axis=0) for share in (gain_a, gain_b, gain_c, gain_d)])
    half = attend_back(at, tie(q1, sent[0]), k1, v1, o1, log1, do1, cosine, sine, 0, split)
    part = (heads_g2.two(half[0]), open_g2.next(half[0]), down_g2.four(half[0]))
    dq1, dk1, dv1 = attend_back(
        at, tie(q1, *part), k1, v1, o1, log1, do1, cosine, sine, split, pairs - split, half
    )
    part = (open_g1.one(dq1), down_g1.one(dq1), heads_g2.next(dq1))
    bundles = [[(low_tokens, [dq1, dk1, dv1])]]
    away, got = link.others(bundles, *part)
    input_grad = heads_back_first(tie(at, away[0]), dq1, dk1, dv1, dr1, heads_one)
    part = (open_g1.two(input_grad), down_g1.two(input_grad))
    sent = link.mine_of(bundles, got, input_grad, *part)
    heads_g1 = link.reduce(link, sent[0], attn_widths)
    (down_g2,) = down_g2.out(sent[0])
    part = (open_g2.three(sent[0]), heads_g2.three(sent[0]))
    part = heads_g1.one(down_g2, *part)
    open_g1.next(part)
    down_g1.next(part)
    open_g2.four(part)
    heads_g2.four(part)
    part = heads_g1.two()
    open_g1.three(part)
    down_g1.three(part)
    output_g2, gate_g2, up_g2 = open_g2.out(part)
    query_g2, key_g2, value_g2 = heads_g2.out(part)
    last = heads_g1.next()
    open_g1.four(last)
    down_g1.four(last)
    gain_grads = link.reduce_gains(gain_grads, half[0], sent[0], part, last, last)
    part = heads_g1.three()
    (down_g1,) = down_g1.out(part)
    output_g1, gate_g1, up_g1 = open_g1.out(part)
    heads_g1.four()
    query_g1, key_g1, value_g1 = heads_g1.out()
    return (
        first_out.reshape(tokens.shape),
        second_out.reshape(tokens.shape),
        input_grad.reshape(tokens.shape),
        query_g1,
        key_g1,
        value_g1,
        output_g1,
        gate_g1,
        up_g1,
        down_g1,
        gain_grads[0],
        gain_grads[1],
        query_g2,
        key_g2,
        value_g2,
        output_g2,
        gate_g2,
        up_g2,
        down_g2,
        gain_grads[2],
        gain_grads[3],
    )


def solution(mesh):
    per_seq = P(("fsdp", "rep"))
    shard = P("fsdp")
    return jax.shard_map(
        functools.partial(body, mesh.shape["fsdp"], mesh.shape["rep"]),
        mesh=mesh,
        in_specs=(per_seq,) * 4 + (shard,) * 18,
        out_specs=(per_seq,) * 3 + (shard,) * 18,
        check_vma=False,
    )
```
